32 devices in a mesh: dp: 4 (over y, x), tm: 8 (over z, core).
Axes of the slice: x: 2, y: 2, z: 4, core: 2. Of those that a mesh axis runs over, the one named last changes fastest.
Arguments:
- frames: bfloat16 [2, 8, 4096, 512], P(None, 'dp', 'tm'), may hold values from -6 to 6
- lengths: int32 [8], P('dp'), may hold values from 409 to 4096, as said below
- norm_gain: float32 [2, 512], replicated, may hold values from 0.5 to 1.5
- norm_bias: float32 [2, 512], replicated, may hold values from -1.75 to 1.75
- qkv_weight: bfloat16 [512, 1536], replicated, may hold values from -0.25 to 0.25
- qv_bias: float32 [2, 512], replicated, may hold values from -3 to 3
- out_weight: bfloat16 [512, 512], replicated, may hold values from -1 to 1
- out_bias: float32 [512], replicated, may hold values from -1.75 to 1.75
- up_weight: bfloat16 [512, 2048], replicated, may hold values from -0.25 to 0.25
- up_bias: float32 [2048], replicated, may hold values from -3 to 3
- down_weight: bfloat16 [2048, 512], replicated, may hold values from -0.125 to 0.125
- down_bias: float32 [512], replicated, may hold values from -1.75 to 1.75
- cotangent: bfloat16 [2, 8, 4096, 512], P(None, 'dp', 'tm'), may hold values from -6 to 6
Outputs:
- mixed_out: bfloat16 [2, 8, 4096, 512], P(None, 'dp', 'tm')
- frames_grad: bfloat16 [2, 8, 4096, 512], P(None, 'dp', 'tm')
- norm_gain_grad: float32 [2, 512], replicated
- norm_bias_grad: float32 [2, 512], replicated
- qkv_weight_grad: float32 [512, 1536], replicated
- qv_bias_grad: float32 [2, 512], replicated
- out_weight_grad: float32 [512, 512], replicated
- out_bias_grad: float32 [512], replicated
- up_weight_grad: float32 [512, 2048], replicated
- up_bias_grad: float32 [2048], replicated
- down_weight_grad: float32 [2048, 512], replicated
- down_bias_grad: float32 [512], replicated
The draws below stay inside these ranges and needn't reach their ends.
Inputs may be any that keep to these rules, and one draw needn't show every extreme that they name: `lengths`: in each group of 2 utterances that share an index of dp, one utterance, drawn from the seed, is 4096 frames long.
All inputs are finite; a program needn't handle non-finite values.
Results may differ from the reference program's by a relative error of at most 0.018.
Values may be sent and summed in bfloat16 or wider, within the bound.
No kernel may reach another device: no remote copies, remote signals or barrier semaphores. Data moves between devices by JAX's collectives and lax.ppermute only.
A program may use at most 384 MiB of HBM per device.

```python
import math
import jax
import jax.numpy as jnp
from jax import lax

D = 512
HEADS = 8
FF = 2048
SEG = 16
LEFT = 30
RC = 4
MEMS = 4
MICRO = 2
UTT_DEV = 2
FRAMES = 4096
BATCH = 8


def draw_lengths(key, part):
    key = jax.random.fold_in(key, 7)
    first_key, second_key = jax.random.split(key)
    base_lengths = jax.random.randint(first_key, (BATCH,), FRAMES // 10, FRAMES + 1)
    groups = BATCH // UTT_DEV
    chosen = jax.random.randint(second_key, (groups,), 0, UTT_DEV)
    slot_ids = jnp.arange(BATCH, dtype=jnp.int32) % UTT_DEV
    owners = jnp.arange(BATCH, dtype=jnp.int32) // UTT_DEV
    longest = slot_ids == chosen[owners]
    return jnp.where(longest, FRAMES, base_lengths).astype(jnp.int32)


def shard_levels(key, dims, shards, least, high):
    level, own = 1.0, jax.random.fold_in(key, 6)
    for dim, shards_of in shards:
        steps = jnp.exp(jax.random.uniform(jax.random.fold_in(own, dim), (shards_of,), jnp.float32, least / len(shards), high / len(shards)))
        level = level * jnp.repeat(steps, dims[dim] // shards_of).reshape([-1 if axis == dim else 1 for axis in range(len(dims))])
    return level


def normal_values(key, shape, scale, most, cuts=(), kind=jnp.bfloat16):
    array = scale * jax.random.normal(key, shape, jnp.float32)
    if cuts:
        array = array * shard_levels(key, shape, cuts, -0.22, 0.18)
    return jnp.clip(array, -most, most).astype(kind)


def setup_inputs(seed: int = 0) -> dict:
    arg_keys = jax.random.split(jax.random.key(seed), 14)
    return {
        "frames": normal_values(arg_keys[0], (MICRO, BATCH, FRAMES, D), 1.0, 6.0, ((1, 4), (2, 8))),
        "lengths": draw_lengths(jax.random.fold_in(arg_keys[13], 71), 0),
        "norm_gain": jnp.clip(1.0 + 0.1 * jax.random.normal(arg_keys[2], (2, D), jnp.float32), 0.5, 1.5),
        "norm_bias": normal_values(arg_keys[3], (2, D), 0.3, 1.75, (), jnp.float32),
        "qkv_weight": normal_values(arg_keys[4], (D, 3 * D), D ** -0.5, 0.25),
        "qv_bias": normal_values(arg_keys[5], (2, D), 0.5, 3.0, (), jnp.float32),
        "out_weight": normal_values(arg_keys[6], (D, D), (D // 16) ** -0.5, 1.0),
        "out_bias": normal_values(arg_keys[7], (D,), 0.3, 1.75, (), jnp.float32),
        "up_weight": normal_values(arg_keys[8], (D, FF), D ** -0.5, 0.25),
        "up_bias": normal_values(arg_keys[9], (FF,), 0.5, 3.0, (), jnp.float32),
        "down_weight": normal_values(arg_keys[10], (FF, D), FF ** -0.5, 0.125),
        "down_bias": normal_values(arg_keys[11], (D,), 0.3, 1.75, (), jnp.float32),
        "cotangent": normal_values(arg_keys[12], (MICRO, BATCH, FRAMES, D), 1.0, 6.0, ((1, 4), (2, 8))),
    }


@jax.custom_vjp
def low(v):
    return lax.optimization_barrier(v.astype(jnp.bfloat16)).astype(jnp.float32)

@jax.custom_vjp
def low_back(v):
    return v

def low_keep(v):
    return (low(v), None)

def low_pass(kept, grad):
    return (grad,)

def back_keep(v):
    return (v, None)

def back_low(kept, grad):
    return (low(grad),)
low.defvjp(low_keep, low_pass)
low_back.defvjp(back_keep, back_low)
highest_precision = lax.Precision.HIGHEST

def layer_norm(values, norm_scale, norm_shift):
    center = values - lax.optimization_barrier(jnp.mean(values, axis=-1, keepdims=True))
    spread = lax.optimization_barrier(jnp.mean(center * center, axis=-1, keepdims=True))
    return center * lax.rsqrt(spread + 1e-05) * norm_scale + norm_shift

def project(values, matrix):
    return jnp.einsum('...d,de->...e', values, matrix, precision=highest_precision)

def split_heads(values):
    return values.reshape(values.shape[:-1] + (HEADS, values.shape[-1] // HEADS))

def near_window(extended, segments):
    lead_blocks = -(-LEFT // SEG)
    rows_count = extended.shape[0]
    width = extended.shape[-1]
    blocks = extended.reshape(rows_count, lead_blocks + segments + 1, SEG, width)
    stacked = jnp.stack([blocks[:, shift_index:shift_index + segments] for shift_index in range(lead_blocks + 2)], 2)
    flat = stacked.reshape(rows_count, segments, (lead_blocks + 2) * SEG, width)
    offset = lead_blocks * SEG - LEFT
    return flat[:, :, offset:offset + LEFT + SEG + RC]

def masked_softmax(scores, key_mask):
    keep_mask = key_mask[:, :, None, None, :]
    shifted = jnp.where(keep_mask, scores, -1000000000.0)
    largest = lax.optimization_barrier(jnp.max(shifted, axis=-1, keepdims=True))
    raised = jnp.exp(shifted - largest)
    return raised / lax.optimization_barrier(jnp.sum(raised, axis=-1, keepdims=True))

def attend(queries, keys_in, values_in, key_mask):
    scale_factor = (queries.shape[-1] // HEADS) ** (-0.5)
    scores = jnp.einsum('unqhe,unkhe->unhqk', split_heads(queries), split_heads(keys_in), precision=highest_precision) * scale_factor
    scores = low_back(scores)
    weights = low(masked_softmax(scores, key_mask))
    mixed = jnp.einsum('unhqk,unkhe->unqhe', weights, split_heads(values_in), precision=highest_precision)
    return low(low_back(mixed.reshape(queries.shape)))

def emformer_layer(inputs, lengths, params):
    norm_gain, norm_bias, qkv_weight, qv_bias, out_weight, out_bias, up_weight, up_bias, down_weight, down_bias = params
    width = inputs.shape[-1]
    rows_count = inputs.shape[0]
    segments = inputs.shape[1]
    total_frames = segments * SEG
    w_query = qkv_weight[:, :width]
    w_key = qkv_weight[:, width:2 * width]
    w_value = qkv_weight[:, 2 * width:]
    normed = layer_norm(inputs, norm_gain[0], norm_bias[0])
    normed_low = low(normed)
    queries = low(low_back(project(normed_low, w_query) + qv_bias[0]))
    keys_own = low(low_back(project(normed_low, w_key)))
    values_own = low(low_back(project(normed_low, w_value) + qv_bias[1]))
    pooled = lax.optimization_barrier(jnp.mean(normed, axis=2))
    pooled_query = low(low_back(project(low(pooled), w_query) + qv_bias[0]))
    seg_ids = jnp.arange(segments, dtype=jnp.int32)
    lead_blocks = -(-LEFT // SEG)
    front_rows = jnp.zeros((rows_count, lead_blocks * SEG, width), jnp.float32)
    back_rows = jnp.zeros((rows_count, SEG, width), jnp.float32)

    def extend(rows):
        return jnp.concatenate([front_rows, rows.reshape(rows_count, total_frames, width), back_rows], 1)
    near_keys = near_window(extend(keys_own), segments)
    near_values = near_window(extend(values_own), segments)
    window_ids = seg_ids[:, None] * SEG - LEFT + jnp.arange(LEFT + SEG + RC, dtype=jnp.int32)[None, :]
    inside = (window_ids >= 0) & (window_ids < total_frames)
    near_valid = inside[None] & ((window_ids[None] < lengths[:, None, None]) | (window_ids % SEG == 0)[None])
    summary = attend(pooled_query[:, :, None], near_keys, near_values, near_valid)[:, :, 0]
    memory = low(low_back(project(summary, out_weight) + out_bias))
    memory_keys = low(low_back(project(memory, w_key)))
    memory_values = low(low_back(project(memory, w_value) + qv_bias[1]))
    blank_bank = jnp.zeros((rows_count, MEMS, width), jnp.float32)
    padded_keys = jnp.concatenate([blank_bank, memory_keys], 1)
    padded_values = jnp.concatenate([blank_bank, memory_values], 1)
    window_keys = jnp.stack([padded_keys[:, slot_index:slot_index + segments] for slot_index in range(MEMS)], 2)
    window_values = jnp.stack([padded_values[:, slot_index:slot_index + segments] for slot_index in range(MEMS)], 2)
    slots = jnp.arange(MEMS, dtype=jnp.int32)
    window_valid = jnp.broadcast_to((seg_ids[:, None] - MEMS + slots[None, :] >= 0)[None], (rows_count, segments, MEMS))
    all_keys = jnp.concatenate([window_keys, near_keys], 2)
    all_values = jnp.concatenate([window_values, near_values], 2)
    all_valid = jnp.concatenate([window_valid, near_valid], 2)
    attended = attend(queries, all_keys, all_values, all_valid)
    mixed = inputs + low_back(project(attended, out_weight) + out_bias)
    normed_two = layer_norm(mixed, norm_gain[1], norm_bias[1])
    upper = low_back(project(low(normed_two), up_weight) + up_bias)
    activated = low(jax.nn.gelu(upper, approximate=False))
    return mixed + project(activated, down_weight) + down_bias

def reference(frames, lengths, norm_gain, norm_bias, qkv_weight, qv_bias, out_weight, out_bias, up_weight, up_bias, down_weight, down_bias, cotangent):
    params = tuple((weight_arg.astype(jnp.float32) for weight_arg in (norm_gain, norm_bias, qkv_weight, qv_bias, out_weight, out_bias, up_weight, up_bias, down_weight, down_bias)))
    segments = FRAMES // SEG
    group = math.gcd(BATCH, max(1, 4096 // FRAMES))
    blocks = BATCH // group
    inputs = frames.astype(jnp.float32).reshape(MICRO * blocks, group, segments, SEG, D)
    grads_in = cotangent.astype(jnp.float32).reshape(MICRO * blocks, group, segments, SEG, D)
    length_rows = jnp.tile(lengths.reshape(blocks, group), (MICRO, 1))

    def step_block(totals, entries):
        block_inputs, block_grads, block_lengths = entries

        def apply_layer(values, *weights):
            return emformer_layer(values, block_lengths, weights)
        outputs, pullback = jax.vjp(apply_layer, block_inputs, *params)
        cotangents = pullback(block_grads)
        totals = tuple((total + part_grad for total, part_grad in zip(totals, cotangents[1:])))
        return (totals, (outputs.astype(jnp.bfloat16), cotangents[0].astype(jnp.bfloat16)))
    initial = tuple((jnp.zeros_like(weight_arg) for weight_arg in params))
    totals, (outputs, input_grads) = lax.scan(step_block, initial, (inputs, grads_in, length_rows))
    shape_full = (MICRO, BATCH, FRAMES, D)
    return (outputs.reshape(shape_full), input_grads.reshape(shape_full), totals[0], totals[1], totals[2], totals[3], totals[4], totals[5], totals[6], totals[7], totals[8], totals[9])
```

```python
import functools

import jax
import jax.numpy as jnp
import numpy as np
from jax import lax
from jax.experimental import pallas as pl
from jax.experimental.pallas import tpu as pltpu
from jax.sharding import PartitionSpec as P

HEADS = 8
SEG = 16
LEFT = 30
RC = 4
MEMS = 4
D = 512
HD = D // HEADS
GROUP = 4
GQ = GROUP * SEG
NEAR = 112
MEMK = 16
KEYS = MEMK + NEAR
HL = 96
HR = 16
HALO = HL + HR
OWN0 = HL - 32
SCALE = HD**-0.5
NEG = -1000000000.0
MB = 1024 * 1024

f32 = jnp.float32
bf16 = jnp.bfloat16


def dot(a, b):
    return lax.dot_general(a, b, (((1,), (0,)), ((), ())), preferred_element_type=f32)


def dot_nt(a, b):
    return lax.dot_general(a, b, (((1,), (1,)), ((), ())), preferred_element_type=f32)


def dot_tn(a, b):
    return lax.dot_general(a, b, (((0,), (0,)), ((), ())), preferred_element_type=f32)


def normalize(x):
    center = x - jnp.mean(x, axis=-1, keepdims=True)
    spread = jnp.mean(center * center, axis=-1, keepdims=True)
    r = lax.rsqrt(spread + 1e-05)
    return center * r, r


def norm_back(grad_y, n, r, gain):
    d = grad_y * gain
    return r * (d - jnp.mean(d, axis=-1, keepdims=True) - n * jnp.mean(d * n, axis=-1, keepdims=True))


def col_sum(v):
    return jnp.sum(v, axis=0, keepdims=True)


def row_blocks(rows, most):
    size = max(d for d in range(16, most + 1, 16) if rows % d == 0)
    return [slice(r0, r0 + size) for r0 in range(0, rows, size)]


def fold_rows(v, op=jnp.sum):
    return op(v.reshape(-1, 8, v.shape[-1]), axis=0)


def block_diag(rows, masks):
    return jnp.concatenate([rows * m for m in masks], 0)


def pick_heads(r, rows):
    lane = lax.broadcasted_iota(jnp.int32, (rows, 128), 1)
    return jnp.where(lane < HD, r[:rows], r[rows:])


def valid_frames(f, total, length):
    return (f >= 0) & (f < total) & ((f < length) | ((f & (SEG - 1)) == 0))


def softmax_rows(s):
    m = jnp.max(s, axis=0, keepdims=True)
    e = jnp.exp(s - m)
    return e * (1.0 / jnp.sum(e, axis=0, keepdims=True))


def const_spec(shape):
    zeros = (0,) * len(shape)
    return pl.BlockSpec(shape, lambda r: zeros, pipeline_mode=pl.Buffered(1))


def row_spec(shape):
    zeros = (0,) * len(shape)
    return pl.BlockSpec((1,) + shape, lambda r: (r,) + zeros)


def in_vmem(shape, dtype):
    return pltpu.VMEM(shape, dtype)


def smem_spec():
    return pl.BlockSpec(memory_space=pltpu.SMEM)


def params(mb=60):
    return pltpu.CompilerParams(dimension_semantics=("arbitrary",), vmem_limit_bytes=mb * MB)


def cost():
    return pl.CostEstimate(flops=1000000, bytes_accessed=100000, transcendentals=0)


def own_kernel(
    x_ref,
    gain_ref,
    bias_ref,
    w_ref,
    qvb_ref,
    pool_ref,
    q_ref,
    k_ref,
    v_ref,
    nt_ref,
    ns_ref,
    pooled_ref,
    pq_ref,
    low_s,
    n_s,
):
    t = x_ref.shape[1]
    for rows in row_blocks(t, 32):
        n, _ = normalize(x_ref[0, rows].astype(f32))
        low_s[rows] = (n * gain_ref[0:1] + bias_ref[0:1]).astype(bf16)
        n_s[rows] = n.astype(bf16)
    low = low_s[...]
    q_ref[0] = ((dot(low, w_ref[:, :D]) + qvb_ref[0:1]) * SCALE).astype(bf16)
    for rows in row_blocks(t, 128):
        nt_ref[0, :, rows] = n_s[rows].T
    k_ref[0, HL : HL + t] = dot(low, w_ref[:, D : 2 * D]).astype(bf16)
    v_ref[0, HL : HL + t] = (dot(low, w_ref[:, 2 * D :]) + qvb_ref[1:2]).astype(bf16)
    ns_ref[0] = dot(pool_ref[...], n_s[...])
    pooled = (dot(pool_ref[...], low) * (1.0 / SEG)).astype(bf16)
    pooled_ref[0] = pooled
    pq_ref[0] = ((dot(pooled, w_ref[:, :D]) + qvb_ref[0:1]) * SCALE).astype(bf16)


def near_mask(keys, lanes, seg_mask, seg0, frame0, position, total, length):
    f = lax.broadcasted_iota(jnp.int32, (keys, lanes), 0) + frame0
    seg = (lax.broadcasted_iota(jnp.int32, (keys, lanes), 1) & seg_mask) + seg0
    start = seg * SEG
    ok = (f >= start - LEFT) & (f < start + (SEG + RC))
    return ok & valid_frames(f + position, total, length)


def memory_kernel(
    groups,
    total,
    utts,
    len_ref,
    xl_ref,
    xr_ref,
    pq_ref,
    gain_ref,
    bias_ref,
    w_ref,
    qvb_ref,
    ow_ref,
    ob_ref,
    poolh_ref,
    expand_ref,
    hm8_ref,
    kin_ref,
    vin_ref,
    q_ref,
    hm4_ref,
    inside_ref,
    kext_ref,
    vext_ref,
    mkg_hbm,
    mvg_hbm,
    summary_hbm,
    memory_hbm,
    ps_hbm,
    p_ref,
    att_ref,
    k_s,
    v_s,
    score_s,
    prob_s,
    mkg_ref,
    mvg_ref,
    summary_ref,
    memory_ref,
    ps_ref,
    in_sem,
    out_sem,
    early_sem,
):
    step = pl.program_id(0)
    early_refs = (mkg_hbm, mvg_hbm, summary_hbm, memory_hbm, ps_hbm)

    @pl.when(step == pl.num_programs(0) - 1)
    def _():
        for value, out, sem in zip((mkg_ref, mvg_ref, summary_ref, memory_ref, ps_ref), early_refs, range(5)):
            pltpu.make_async_copy(value, out, early_sem.at[sem]).wait()

    @pl.when(step == 0)
    def _():
        memory_step(
            total,
            utts,
            len_ref,
            xl_ref,
            xr_ref,
            pq_ref,
            gain_ref,
            bias_ref,
            w_ref,
            qvb_ref,
            ow_ref,
            ob_ref,
            poolh_ref,
            expand_ref,
            hm8_ref,
            kin_ref,
            vin_ref,
            kext_ref,
            vext_ref,
            mkg_ref,
            mvg_ref,
            summary_ref,
            memory_ref,
            ps_ref,
            k_s,
            v_s,
            score_s,
            prob_s,
            in_sem,
            out_sem,
            early_refs,
            early_sem,
        )

    @pl.when(step > 0)
    def _():
        row = step - 1
        attend_step(
            groups,
            total,
            len_ref[lax.rem(row, utts)],
            q_ref,
            k_s.at[pl.ds(row, 1)],
            v_s.at[pl.ds(row, 1)],
            mkg_ref.at[pl.ds(row, 1)],
            mvg_ref.at[pl.ds(row, 1)],
            hm4_ref,
            inside_ref,
            p_ref,
            att_ref,
        )


def memory_step(
    total,
    utts,
    len_ref,
    xl_ref,
    xr_ref,
    pq_ref,
    gain_ref,
    bias_ref,
    w_ref,
    qvb_ref,
    ow_ref,
    ob_ref,
    poolh_ref,
    expand_ref,
    hm8_ref,
    kin_ref,
    vin_ref,
    kext_ref,
    vext_ref,
    mkg_ref,
    mvg_ref,
    summary_ref,
    memory_ref,
    ps_ref,
    k_s,
    v_s,
    score_s,
    prob_s,
    in_sem,
    out_sem,
    early_refs,
    early_sem,
):
    rows, ext, _ = k_s.shape
    t = ext - HALO
    sp = pq_ref.shape[1]
    own_keys = ext - OWN0
    loads = [pltpu.make_async_copy(kin_ref, k_s, in_sem.at[0]), pltpu.make_async_copy(vin_ref, v_s, in_sem.at[1])]
    for load in loads:
        load.start()
    position = lax.axis_index("tm") * t
    halo = [xl_ref[...].reshape(rows * HL, D), xr_ref[...].reshape(rows * HR, D)]
    n, _ = normalize(jnp.concatenate(halo, 0).astype(f32))
    low = (n * gain_ref[0:1] + bias_ref[0:1]).astype(bf16)
    kh = dot(low, w_ref[:, D : 2 * D]).astype(bf16)
    vh = (dot(low, w_ref[:, 2 * D :]) + qvb_ref[1:2]).astype(bf16)
    pooled = [dot(poolh_ref[...], low[r * HL : (r + 1) * HL]) * (1.0 / SEG) for r in range(rows)]
    pooled = jnp.concatenate(pooled, 0).astype(bf16)
    pqh = ((dot(pooled, w_ref[:, :D]) + qvb_ref[0:1]) * SCALE).astype(bf16)
    for load in loads:
        load.wait()
    for scratch, value in ((k_s, kh), (v_s, vh)):
        for r in range(rows):
            scratch[r, :HL] = value[r * HL : (r + 1) * HL]
            scratch[r, HL + t :] = value[rows * HL + r * HR : rows * HL + (r + 1) * HR]
    stores = []
    for i, (scratch, out) in enumerate(((k_s, kext_ref), (v_s, vext_ref))):
        for j, part in enumerate((pl.ds(0, HL), pl.ds(HL + t, HR))):
            stores.append(pltpu.make_async_copy(scratch.at[:, part], out.at[:, part], out_sem.at[2 * i + j]))
    for store in stores:
        store.start()
    masks8 = [hm8_ref[h : h + 1] for h in range(HEADS)]
    jobs = []
    for r in range(rows):
        jobs.append((r, slice(0, HALO), 16, -16, -HL))
        jobs.append((r, slice(OWN0, ext), sp, 0, -32))
    sums = []
    for step in range(len(jobs) + 2):
        if step < len(jobs):
            r, keys, count, _, _ = jobs[step]
            pq = pqh[r * 16 : (r + 1) * 16] if step % 2 == 0 else pq_ref[r]
            score_s[step % 4, : keys.stop - keys.start, : HEADS * count] = dot_nt(k_s[r, keys], block_diag(pq, masks8))
        if 1 <= step <= len(jobs):
            r, keys, count, seg0, frame0 = jobs[step - 1]
            score, prob = score_s.at[(step - 1) % 4], prob_s.at[(step - 1) % 4]
            blocks = row_blocks(keys.stop - keys.start, 128)
            for l0 in range(0, HEADS * count, 128):
                lanes = slice(l0, l0 + 128)
                most = None
                for block in blocks:
                    shape = (block.stop - block.start, 128)
                    mask = near_mask(*shape, count - 1, seg0, frame0 + block.start, position, total, len_ref[r % utts])
                    value = jnp.where(mask, score[block, lanes], NEG)
                    score[block, lanes] = value
                    value = fold_rows(value, jnp.max)
                    most = value if most is None else jnp.maximum(most, value)
                most = jnp.max(most, axis=0, keepdims=True)
                weight = 0.0
                for block in blocks:
                    value = jnp.exp(score[block, lanes] - most)
                    score[block, lanes] = value
                    weight += fold_rows(value)
                weight = 1.0 / col_sum(weight)
                for block in blocks:
                    value = (score[block, lanes] * weight).astype(bf16)
                    prob[block, lanes] = value
                    if step % 2 == 0:
                        ps_ref[r, block, lanes] = value
        if step >= 2:
            r, keys, count, _, _ = jobs[step - 2]
            prob = prob_s[(step - 2) % 4, : keys.stop - keys.start, : HEADS * count]
            o = dot_tn(prob, v_s[r, keys])
            o = [
                pick_heads(o[2 * j * count : (2 * j + 2) * count, 128 * j : 128 * j + 128], count)
                for j in range(HEADS // 2)
            ]
            sums.append(jnp.concatenate(o, 1).astype(bf16))
            if step % 2:
                summary_ref[r] = sums[-1]
    memory = (dot(jnp.concatenate(sums, 0), ow_ref[...]) + ob_ref[...]).astype(bf16)
    mk = dot(memory, w_ref[:, D : 2 * D]).astype(bf16)
    mv = (dot(memory, w_ref[:, 2 * D :]) + qvb_ref[1:2]).astype(bf16)
    both = jnp.concatenate([mk, mv], 1)
    for r in range(rows):
        here = slice(r * (16 + sp), (r + 1) * (16 + sp))
        memory_ref[r] = memory[here][16:]
        spread = dot(expand_ref[...], both[here]).astype(bf16)
        mkg_ref[r] = spread[:, :D]
        mvg_ref[r] = spread[:, D:]
    for value, out, sem in zip((mkg_ref, mvg_ref, summary_ref, memory_ref, ps_ref), early_refs, range(5)):
        pltpu.make_async_copy(value, out, early_sem.at[sem]).start()
    for store in stores:
        store.wait()


def group_keys(ref, mem_ref, g):
    k0 = g * GQ + OWN0
    return jnp.concatenate([mem_ref[0, g * MEMK : (g + 1) * MEMK], ref[0, k0 : k0 + NEAR]], 0)


def attend_step(
    groups, total, length, q_ref, kext_ref, vext_ref, mkg_ref, mvg_ref, hm4_ref, inside_ref, p_ref, att_ref
):
    position = lax.axis_index("tm") * q_ref.shape[1]
    masks4 = [hm4_ref[h : h + 1] for h in range(4)]
    slot = lax.broadcasted_iota(jnp.int32, (KEYS, 128), 0)
    inside = inside_ref[...] > 0.5
    scores, probs = {}, {}
    for step in range(groups + 2):
        if step < groups:
            g = step
            q = q_ref[0, g * GQ : (g + 1) * GQ]
            kc = group_keys(kext_ref, mkg_ref, g)
            for quad in range(2):
                c0 = 256 * quad
                scores[g, quad] = dot_nt(kc[:, c0 : c0 + 256], block_diag(q[:, c0 : c0 + 256], masks4))
        if 1 <= step <= groups:
            g = step - 1
            f = jnp.where(slot < MEMK, (slot + (g * GROUP - MEMS)) * SEG, slot + (g * GQ - 32 - MEMK)) + position
            keep = inside & valid_frames(f, total, length)
            for pair in range(HEADS // 2):
                cp = 128 * pair
                s = scores[g, pair // 2][:, 128 * (pair % 2) : 128 * (pair % 2) + 128]
                probs[g, pair] = softmax_rows(jnp.where(keep, s, NEG)).astype(bf16)
                p_ref[0, g, :, cp : cp + 128] = probs[g, pair]
        if step >= 2:
            g = step - 2
            vc = group_keys(vext_ref, mvg_ref, g)
            for pair in range(HEADS // 2):
                cp = 128 * pair
                r = dot_tn(probs[g, pair], vc[:, cp : cp + 128])
                att_ref[0, g * GQ : (g + 1) * GQ, cp : cp + 128] = pick_heads(r, GQ).astype(bf16)


def split_halves(bit_ref, keep_ref, send_ref, cols, src_ref):
    half = D // 2

    @pl.when(bit_ref[0] == 0)
    def _():
        keep_ref[:, cols] = src_ref[:half].astype(bf16)
        send_ref[:, cols] = src_ref[half:].astype(bf16)

    @pl.when(bit_ref[0] != 0)
    def _():
        keep_ref[:, cols] = src_ref[half:].astype(bf16)
        send_ref[:, cols] = src_ref[:half].astype(bf16)


def gelu_both(v):
    e = jnp.exp2(v * v * (-0.5 * 1.4426950408889634))
    t = pl.reciprocal(1.0 + jnp.abs(v) * (0.3275911 * 0.5**0.5), approx=True)
    e, t, v = e.astype(bf16), t.astype(bf16), v.astype(bf16)
    poly = 0.5 * -1.453152027 + t * (0.5 * 1.061405429)
    poly = 0.5 * 1.421413741 + t * poly
    poly = 0.5 * -0.284496736 + t * poly
    poly = 0.5 * 0.254829592 + t * poly
    tail = t * poly * e
    phi = jnp.where(v >= 0, 1 - tail, tail)
    return v * phi, phi + v * (e * 0.3989422804014327)


def ff_kernel(
    tiles,
    bit_ref,
    x_ref,
    c_ref,
    att_ref,
    gain_ref,
    bias_ref,
    ow_ref,
    ob_ref,
    uw_ref,
    ub_ref,
    dw_ref,
    db_ref,
    out_ref,
    gmix_ref,
    gatt_ref,
    keep_ref,
    send_ref,
    outg_ref,
    vec_ref,
    upb_ref,
    n_s,
    r_s,
    n2_s,
    n2t_s,
    ct_s,
    up0_s,
    up1_s,
    da0_s,
    da1_s,
    act0_s,
    act1_s,
    dup0_s,
    dup1_s,
    acc_s,
    gy_s,
    upg_s,
    dng_s,
):
    step = pl.program_id(0)
    ff = uw_ref.shape[1]
    wide = ff // tiles
    up_s, da_s, act_s, dup_s = (up0_s, up1_s), (da0_s, da1_s), (act0_s, act1_s), (dup0_s, dup1_s)

    @pl.when(step == 0)
    def _():
        upg_s[...] = jnp.zeros_like(upg_s)
        dng_s[...] = jnp.zeros_like(dng_s)
        outg_ref[...] = jnp.zeros_like(outg_ref)
        vec_ref[...] = jnp.zeros_like(vec_ref)
        upb_ref[...] = jnp.zeros_like(upb_ref)

    gy_s[...] = x_ref[...].astype(f32) + dot(att_ref[...], ow_ref[...]) + ob_ref[...]
    for rows in row_blocks(x_ref.shape[0], 32):
        mixed = gy_s[rows]
        n, r = normalize(mixed)
        n_s[rows] = n
        r_s[rows] = jnp.broadcast_to(r, (mixed.shape[0], 128))
        n2_s[rows] = (n * gain_ref[1:2] + bias_ref[1:2]).astype(bf16)
        acc_s[rows] = mixed + db_ref[...]
    for rows in row_blocks(x_ref.shape[0], 128):
        n2t_s[:D, rows] = n2_s[rows].T
        ct_s[:, rows] = c_ref[rows].T
    n2t_s[D:] = jnp.ones((16, x_ref.shape[0]), bf16)

    tb = x_ref.shape[0]
    chunk = min(512, tb)

    def gelu_rows(i, few):
        half = slice((i % 2) * wide, (i % 2 + 1) * wide)
        act, slope = gelu_both(up_s[i % 2][few])
        act_s[i // 2 % 2][few, half] = act
        dup_s[i // 2 % 2][few, half] = slope * da_s[i % 2][few]

    for j in range(tiles + 2):
        pieces = row_blocks(tb, 64) if 1 <= j <= tiles else []

        def some(count):
            for few in pieces[:count]:
                gelu_rows(j - 1, few)
            del pieces[:count]

        for r0 in range(0, tb, chunk):
            rows = slice(r0, r0 + chunk)
            if j < tiles:
                cols = slice(j * wide, (j + 1) * wide)
                up_s[j % 2][rows] = dot(n2_s[rows], uw_ref[:, cols]) + ub_ref[:, cols]
                some(3)
                da_s[j % 2][rows] = dot_nt(c_ref[rows], dw_ref[cols, :]).astype(bf16)
            some(3)
            if j >= 2 and j % 2:
                i = j - 2
                both = slice((i - 1) * wide, (i + 1) * wide)
                acc_s[rows] += dot(act_s[i // 2 % 2][rows], dw_ref[both, :])
                back = dot_nt(dup_s[i // 2 % 2][rows], uw_ref[:, both])
                gy_s[rows] = back if i == 1 else gy_s[rows] + back
        some(len(pieces))
        if j >= 2:
            i = j - 2
            cols = slice(i * wide, (i + 1) * wide)
            half = slice((i % 2) * wide, (i % 2 + 1) * wide)
            grad = dot(n2t_s[...], dup_s[i // 2 % 2][:, half])
            upg_s[:, cols] += grad[:D]
            upb_ref[:, cols] += grad[D : D + 1]
            dng_s[:, cols] += dot(ct_s[...], act_s[i // 2 % 2][:, half])

    sums = [0.0] * 4
    for rows in row_blocks(x_ref.shape[0], 32):
        out_ref[rows] = acc_s[rows].astype(bf16)
        n = n_s[rows]
        cf = c_ref[rows].astype(f32)
        gy = gy_s[rows]
        gmix = cf + norm_back(gy, n, r_s[rows, 0:1], gain_ref[1:2])
        gmix_ref[rows] = gmix.astype(bf16)
        sums = [a + fold_rows(b) for a, b in zip(sums, (gy * n, gy, gmix, cf))]
    branch = gmix_ref[...]
    gatt_ref[...] = dot_nt(branch, ow_ref[...]).astype(bf16)
    outg_ref[...] += dot_tn(att_ref[...], branch)
    for i, value in enumerate(sums):
        vec_ref[i : i + 1] += col_sum(value)

    @pl.when(step == pl.num_programs(0) - 1)
    def _():
        split_halves(bit_ref, keep_ref, send_ref, slice(0, ff), upg_s)
        split_halves(bit_ref, keep_ref, send_ref, slice(ff, 2 * ff), dng_s)


def attend_back_kernel(
    g0,
    g1,
    q_ref,
    kext_ref,
    vext_ref,
    mkg_ref,
    mvg_ref,
    p_ref,
    g_ref,
    hm4_ref,
    dq_ref,
    dk_ref,
    dv_ref,
    dm_ref,
    first_ref,
    dk_s,
    dv_s,
):
    dk_s[...] = jnp.zeros_like(dk_s)
    dv_s[...] = jnp.zeros_like(dv_s)
    masks4 = [hm4_ref[h : h + 1] for h in range(4)]
    count = g1 - g0
    grads, backs = {}, {}
    for step in range(count + 2):
        if step < count:
            g = step
            go = g_ref[0, (g0 + g) * GQ : (g0 + g + 1) * GQ]
            vc = group_keys(vext_ref, mvg_ref, g0 + g)
            for quad in range(2):
                cols = slice(256 * quad, 256 * quad + 256)
                grads[g, quad] = dot_nt(vc[:, cols], block_diag(go[:, cols], masks4))
        if 1 <= step <= count:
            g = step - 1
            for pair in range(HEADS // 2):
                half = slice(128 * (pair % 2), 128 * (pair % 2) + 128)
                p = p_ref[0, g0 + g, :, 128 * pair : 128 * pair + 128].astype(f32)
                pdp = p * grads[g, pair // 2][:, half]
                backs[g, pair] = (pdp - p * col_sum(pdp)).astype(bf16)
        if step >= 2:
            g = step - 2
            here = slice(g * GQ, (g + 1) * GQ)
            near = slice(g * GQ, g * GQ + NEAR)
            mem = slice(g * MEMK, (g + 1) * MEMK)
            there = slice((g0 + g) * GQ, (g0 + g + 1) * GQ)
            q = q_ref[0, there]
            go = g_ref[0, there]
            kc = group_keys(kext_ref, mkg_ref, g0 + g)
            for quad in range(2):
                c0 = 256 * quad
                cols = slice(c0, c0 + 256)
                dv_cols = slice(D + c0, D + c0 + 256)
                ds = jnp.concatenate([backs[g, 2 * quad], backs[g, 2 * quad + 1]], 1)
                dv = dot(p_ref[0, g0 + g, :, cols], block_diag(go[:, cols], masks4))
                dk = dot(ds, block_diag(q[:, cols], masks4))
                dm_ref[0, mem, cols] = dk[:MEMK].astype(bf16)
                dm_ref[0, mem, dv_cols] = dv[:MEMK].astype(bf16)
                if g0 + g == 0:
                    first_ref[0, :, cols] = dk[:MEMK].astype(bf16)
                    first_ref[0, :, dv_cols] = dv[:MEMK].astype(bf16)
                dk_s[near, cols] += dk[MEMK:]
                dv_s[near, cols] += dv[MEMK:]
                for pair in range(2):
                    cp = c0 + 128 * pair
                    r = dot_tn(backs[g, 2 * quad + pair], kc[:, cp : cp + 128])
                    dq_ref[0, here, cp : cp + 128] = (pick_heads(r, GQ) * SCALE).astype(bf16)
    dk_ref[0] = dk_s[...].astype(bf16)
    dv_ref[0] = dv_s[...].astype(bf16)
    if g0:
        first_ref[...] = jnp.zeros_like(first_ref)


def memory_back_kernel(parts, *refs):
    count = len(parts)
    dm_refs, main_hbm = refs[:count], refs[count : 3 * count]
    (
        recv_ref,
        fold_ref,
        place_ref,
        w_ref,
        ow_ref,
        hm8_ref,
        pq_ref,
        kext_hbm,
        vext_hbm,
        ps_hbm,
        dko_hbm,
        dvo_hbm,
        left_ref,
        right_ref,
        gpq_ref,
        dmo_ref,
        gm_ref,
        k_s,
        v_s,
        ps_s,
        dp_s,
        ds_s,
        dk_s,
        dv_s,
        dko_s,
        dvo_s,
        *main_s,
        in_sems,
        out_sems,
    ) = refs[3 * count :]
    rows, sp, _ = pq_ref.shape
    t = dko_s.shape[1]
    own = pl.ds(OWN0, k_s.shape[1])
    loads = []
    for r in range(rows):
        pairs = [(vext_hbm.at[r, own], v_s.at[r]), (ps_hbm.at[r], ps_s.at[r]), (kext_hbm.at[r, own], k_s.at[r])]
        pairs += [(src.at[r], held.at[r]) for src, held in zip(main_hbm, main_s)]
        loads.append([pltpu.make_async_copy(src, dst, in_sems.at[r, i]) for i, (src, dst) in enumerate(pairs)])
    for row in loads:
        for load in row:
            load.start()
    stores = []
    for r in range(rows):
        pairs = ((dko_s.at[r], dko_hbm.at[r]), (dvo_s.at[r], dvo_hbm.at[r]))
        stores.append([pltpu.make_async_copy(src, dst, out_sems.at[r, i]) for i, (src, dst) in enumerate(pairs)])
    masks8 = [hm8_ref[h : h + 1] for h in range(HEADS)]

    def fold(r):
        got = dot(fold_ref[...], jnp.concatenate([ref[r] for ref in dm_refs], 0))
        return (got + dot(place_ref[...], recv_ref[r])).astype(bf16)

    dm = jnp.concatenate([fold(r) for r in range(rows)], 0)
    gm = dot_nt(dm, w_ref[:, D:]).astype(bf16)
    gs = dot_nt(gm, ow_ref[...]).astype(bf16)
    for r in range(rows):
        dmo_ref[r] = dm[r * sp : (r + 1) * sp]
        gm_ref[r] = gm[r * sp : (r + 1) * sp]
    gbd = {}
    blocks = row_blocks(dp_s.shape[1], 128)
    for step in range(rows + 2):
        if step < rows:
            loads[step][0].wait()
        if 1 <= step <= rows:
            loads[step - 1][1].wait()
        if step >= 2:
            for load in loads[step - 2][2:]:
                load.wait()
        if step < rows:
            r = step
            gbd[r] = block_diag(gs[r * sp : (r + 1) * sp], masks8)
            dp_s[r] = dot_nt(v_s[r], gbd[r])
        if 1 <= step <= rows:
            r = step - 1
            for l0 in range(0, HEADS * sp, 128):
                lanes = slice(l0, l0 + 128)
                weight = 0.0
                for block in blocks:
                    pdp = ps_s[r, block, lanes].astype(f32) * dp_s[r, block, lanes]
                    dp_s[r, block, lanes] = pdp
                    weight += fold_rows(pdp)
                weight = col_sum(weight)
                for block in blocks:
                    p = ps_s[r, block, lanes].astype(f32)
                    ds_s[r, block, lanes] = (dp_s[r, block, lanes] - p * weight).astype(bf16)
        if step >= 2:
            r = step - 2
            ds = ds_s[r]
            dq = dot_tn(ds, k_s[r])
            dq = [
                pick_heads(dq[2 * j * sp : (2 * j + 2) * sp, 128 * j : 128 * j + 128], sp)
                for j in range(HEADS // 2)
            ]
            gpq_ref[r] = (jnp.concatenate(dq, 1) * SCALE).astype(bf16)
            for left, right, sum_s, held, out_s, cols in (
                (ds, block_diag(pq_ref[r], masks8), dk_s, main_s[:count], dko_s, slice(0, D)),
                (ps_s[r], gbd[r], dv_s, main_s[count:], dvo_s, slice(D, 2 * D)),
            ):
                sum_s[r] = dot(left, right)
                for (g0, _), main in zip(parts, held):
                    sum_s[r, g0 * GQ : g0 * GQ + main.shape[1]] += main[r].astype(f32)
                left_ref[r, :, cols] = sum_s[r, :32].astype(bf16)
                out_s[r] = sum_s[r, 32 : 32 + t].astype(bf16)
                right_ref[r, :, cols] = sum_s[r, 32 + t :].astype(bf16)
            for store in stores[r]:
                store.start()
    for row in stores:
        for store in row:
            store.wait()


def query_weights_kernel(count, nt_ref, ns_ref, *refs):
    dq_refs = refs[:count]
    gpq_ref, w_ref, acc_ref, sum_ref = refs[count:]

    @pl.when(pl.program_id(0) == 0)
    def _():
        acc_ref[...] = jnp.zeros_like(acc_ref)
        sum_ref[...] = jnp.zeros_like(sum_ref)

    dq = jnp.concatenate([ref[0] for ref in dq_refs], 0)
    acc_ref[...] += dot(nt_ref[0], dq)
    gp = dot_nt(gpq_ref[0], w_ref[...]) * (1.0 / SEG)
    sum_ref[0:1] += col_sum(gp * ns_ref[0])
    sum_ref[1:2] += col_sum(gp) * SEG
    sum_ref[2:3] += col_sum(dq.astype(f32))


def shared_frames(main, from_left, from_right):
    t = main.shape[0]
    first = (main[:HR].astype(f32) + from_left.astype(f32)).astype(bf16)
    last = (main[t - 32 :].astype(f32) + from_right.astype(f32)).astype(bf16)
    return jnp.concatenate([first, main[HR : t - 32], last], 0)


def key_weights_kernel(
    nt_ref,
    dk_ref,
    dv_ref,
    fr_ref,
    fl_ref,
    gain_ref,
    bias_ref,
    sum_ref,
    pooled_ref,
    gpq_ref,
    memory_ref,
    dm_ref,
    summary_ref,
    gm_ref,
    vec_ref,
    upb_ref,
    w_hbm,
    accq_hbm,
    outg_hbm,
    bit_ref,
    keep_ref,
    send_ref,
    acc_s,
    cs_s,
    grads_s,
    norm_s,
    w_ref,
    accq_ref,
    outg_ref,
    sems,
):
    row = pl.program_id(0)
    late = ((w_hbm, w_ref), (accq_hbm, accq_ref), (outg_hbm, outg_ref))
    loads = [pltpu.make_async_copy(src, dst, sems.at[i]) for i, (src, dst) in enumerate(late)]

    @pl.when(row == 0)
    def _():
        for load in loads:
            load.start()
        acc_s[...] = jnp.zeros_like(acc_s)
        cs_s[...] = jnp.zeros_like(cs_s)

    for ref, cols in ((dk_ref, slice(0, D)), (dv_ref, slice(D, 2 * D))):
        d = shared_frames(ref[0], fl_ref[0, :, cols], fr_ref[0, :, cols])
        acc_s[:, cols] += dot(nt_ref[0], d)
        cs_s[:, cols] += col_sum(d.astype(f32))

    @pl.when(row == pl.num_programs(0) - 1)
    def _():
        for load in loads:
            load.wait()
        sums = sum_ref[...]
        norm = jnp.concatenate([gain_ref[0:1], bias_ref[0:1], jnp.zeros((126, D), f32)], 0).T
        norm_s[0] = jnp.broadcast_to(norm[:, 0:1], (D, 128))
        norm_s[1] = jnp.broadcast_to(norm[:, 1:2], (D, 128))
        norm_s[2:] = jnp.zeros((2, D, 128), f32)
        for part, (acc_ref, cs, left, right) in enumerate(
            (
                (accq_ref, sums[2:3], pooled_ref[...], gpq_ref[...]),
                (acc_s.at[:, :D], cs_s[:, :D], memory_ref[...], dm_ref[:, :D]),
                (acc_s.at[:, D:], cs_s[:, D:], memory_ref[...], dm_ref[:, D:]),
            )
        ):
            cols = slice(part * D, (part + 1) * D)
            grads_s[...] = dot_tn(left, right)
            for block in row_blocks(D, 128):
                for c0 in range(0, D, 128):
                    lanes = slice(c0, c0 + 128)
                    acc = acc_ref[block, lanes]
                    w = w_ref[block, part * D + c0 : part * D + c0 + 128].astype(f32)
                    grads_s[block, lanes] += acc * norm_s[0, block] + norm_s[1, block] * cs[:, lanes]
                    norm_s[2, block] += w * acc
                    norm_s[3, block] += w * cs[:, lanes]
            split_halves(bit_ref, keep_ref, send_ref, cols, grads_s)
        grads_s[...] = outg_ref[...] + dot_tn(summary_ref[...], gm_ref[...])
        split_halves(bit_ref, keep_ref, send_ref, slice(3 * D, 4 * D), grads_s)
        v = vec_ref[...]
        vectors = [sums[0:1], sums[1:2], v[0:1], v[1:2]]
        vectors += [sums[2:3] + col_sum(gpq_ref[...].astype(f32)), cs_s[:, D:] + col_sum(dm_ref[:, D:].astype(f32))]
        vectors += [v[2:3] + col_sum(gm_ref[...].astype(f32)), v[3:4]]
        hidden = [upb_ref[:, i * D : (i + 1) * D] for i in range(upb_ref.shape[1] // D)]
        packed = vectors + hidden + [jnp.zeros((128 - len(vectors) - len(hidden), D), f32)]
        columns = jnp.concatenate(packed, 0).T
        lane = lax.broadcasted_iota(jnp.int32, columns.shape, 1)
        gain_col = jnp.sum(norm_s[2], axis=-1, keepdims=True)
        bias_col = jnp.sum(norm_s[3], axis=-1, keepdims=True)
        columns += jnp.where(lane == 0, gain_col, jnp.where(lane == 1, bias_col, 0.0))
        grads_s[:, :128] = columns
        split_halves(bit_ref, keep_ref, send_ref, slice(4 * D, 4 * D + 128), grads_s.at[:, :128])


def own_frames_kernel(count, x_ref, *refs):
    dq_refs = refs[:count]
    dk_ref, dv_ref, fr_ref, fl_ref, gpq_ref, gmix_ref, gain_ref, w_ref, fg_ref, gy_s = refs[count:]
    t = x_ref.shape[1]
    gp = (dot_nt(gpq_ref[0], w_ref[:, :D]) * (1.0 / SEG))[: t // SEG]
    spread = jnp.broadcast_to(gp[:, None, :], (t // SEG, SEG, D)).reshape(t, D)
    dq = jnp.concatenate([ref[0] for ref in dq_refs], 0)
    dk = shared_frames(dk_ref[0], fl_ref[0, :, :D], fr_ref[0, :, :D])
    dv = shared_frames(dv_ref[0], fl_ref[0, :, D:], fr_ref[0, :, D:])
    gy_s[...] = (
        dot_nt(dq, w_ref[:, :D]) + dot_nt(dk, w_ref[:, D : 2 * D]) + dot_nt(dv, w_ref[:, 2 * D :]) + spread
    )
    for rows in row_blocks(t, 32):
        n, r = normalize(x_ref[0, rows].astype(f32))
        fg_ref[0, rows] = (gmix_ref[0, rows].astype(f32) + norm_back(gy_s[rows], n, r, gain_ref[0:1])).astype(bf16)


def halves(bit_ref, mine_ref, other_ref, cols):
    first = jnp.where(bit_ref[0] == 0, mine_ref[:, cols], other_ref[:, cols])
    second = jnp.where(bit_ref[0] == 0, other_ref[:, cols], mine_ref[:, cols])
    return jnp.concatenate([first, second], 0).astype(f32)


def unpack_ff_kernel(bit_ref, mine_u, other_u, mine_d, other_d, up_ref, down_ref):
    up_ref[...] = halves(bit_ref, mine_u, other_u, slice(None))
    down_ref[...] = halves(bit_ref, mine_d, other_d, slice(None)).T


def unpack_own_kernel(side_ref, part_ref, qkv_ref, out_ref):
    step = pl.program_id(0)

    @pl.when(step < 3)
    def _():
        qkv_ref[...] = part_ref[...].astype(f32)

    @pl.when(step == 3)
    def _():
        out_ref[...] = part_ref[...].astype(f32)


def unpack_rest_kernel(
    side_ref,
    part_ref,
    mine_v,
    other_v,
    qkv_in,
    out_in,
    qkv_ref,
    out_ref,
    gain_ref,
    bias_ref,
    qvb_ref,
    outb_ref,
    upb_ref,
    downb_ref,
):
    unpack_own_kernel(side_ref, part_ref, qkv_ref, out_ref)

    @pl.when(pl.program_id(0) == 0)
    def _():
        second = side_ref[0] == 1
        first = jnp.where(second, mine_v[...], other_v[...])
        last = jnp.where(second, other_v[...], mine_v[...])
        v = jnp.concatenate([first, last], 0).astype(f32).T
        gain_ref[0:1], gain_ref[1:2] = v[0:1], v[2:3]
        bias_ref[0:1], bias_ref[1:2] = v[1:2], v[3:4]
        qvb_ref[...] = v[4:6]
        outb_ref[...] = v[6:7]
        downb_ref[...] = v[7:8]
        for i in range(upb_ref.shape[1] // D):
            upb_ref[:, i * D : (i + 1) * D] = v[8 + i : 9 + i]


def shifted(value, axis, steps):
    count = lax.axis_size(axis)
    first, last = max(0, -steps), min(count, count - steps)
    return lax.ppermute(value, axis, [(source, source + steps) for source in range(first, last)])


class Exchange:
    def __init__(self):
        self.count_dp, self.count_tm = lax.axis_size("dp"), lax.axis_size("tm")
        dp, tm = lax.axis_index("dp"), lax.axis_index("tm")
        dp_bits = [(1 << b, 0) for b in range(self.count_dp.bit_length() - 1)]
        tm_bits = [(0, 1 << b) for b in range(self.count_tm.bit_length() - 1)]
        self.steps = [([tm_bits[0]], [tm_bits[0]])]
        self.steps += [([a], [b]) for a, b in zip(dp_bits, reversed(dp_bits))]
        self.steps += [(tm_bits[i : i + 2],) * 2 for i in range(1, len(tm_bits), 2)]
        self.digits = []
        for step in self.steps:
            digit = [0, 0]
            for parity in range(2):
                for f_dp, f_tm in step[parity]:
                    one = ((dp & f_dp) + (tm & f_tm) != 0).astype(jnp.int32)
                    digit[parity] = digit[parity] * 2 + one
            self.digits.append(jnp.where((tm & 1) == 0, digit[0], digit[1]))

    def radix(self, index):
        return 1 << len(self.steps[index][0])

    def send(self, part, index, flip=1):
        pairs = []
        for d in range(self.count_dp):
            for t in range(self.count_tm):
                to_d, to_t = d, t
                bits = self.steps[index][t & 1]
                for i, (f_dp, f_tm) in enumerate(bits):
                    if flip >> (len(bits) - 1 - i) & 1:
                        to_d, to_t = to_d ^ f_dp, to_t ^ f_tm
                pairs.append((d * self.count_tm + t, to_d * self.count_tm + to_t))
        return lax.ppermute(part, ("dp", "tm"), pairs)

    def total(self, terms):
        return sum(term.astype(f32) for term in terms).astype(bf16)

    def part(self, terms, index, flip):
        rows = terms[0].shape[0] // self.radix(index)
        start = (self.digits[index] ^ flip) * rows
        return [lax.dynamic_slice_in_dim(term, start, rows) for term in terms]

    def scatter(self, terms, index, sends=None):
        if sends is None:
            sends = [self.total(self.part(terms, index, flip)) for flip in range(1, self.radix(index))]
            terms = self.part(terms, index, 0)
        return terms, [self.send(value, index, flip + 1) for flip, value in enumerate(sends)]

    def gather(self, value, index):
        return [self.send(value, index, flip) for flip in range(1, self.radix(index))]

    def join(self, value, others, index):
        pieces = [value] + others
        out = jnp.concatenate(pieces, 0)
        for digit in range(1, len(pieces)):
            order = [pieces[place ^ digit] for place in range(len(pieces))]
            out = jnp.where(self.digits[index] == digit, jnp.concatenate(order, 0), out)
        return out


class Running:
    def __init__(self, exchange, keep, send):
        self.exchange = exchange
        self.steps = len(exchange.steps)
        self.last = 2 * self.steps - 1
        self.phase = 0
        self.terms, self.arriving = exchange.scatter([keep], 0, [send])
        self.value = None

    def index(self):
        return min(self.phase, self.last - self.phase)

    def beside(self, result):
        self.arriving, _ = lax.optimization_barrier((self.arriving, result))

    def before(self, operand):
        self.arriving, operand = lax.optimization_barrier((self.arriving, operand))
        return operand

    def advance(self):
        if self.phase < self.steps:
            self.terms = self.terms + self.arriving
        else:
            self.value = self.exchange.join(self.value, self.arriving, self.index())
        self.phase += 1
        if self.phase < self.steps:
            self.terms, self.arriving = self.exchange.scatter(self.terms, self.phase)
        else:
            if self.phase == self.steps:
                self.value = self.exchange.total(self.terms)
            self.arriving = self.exchange.gather(self.value, self.index())

    def along(self, result, operand):
        if self.phase < self.last:
            self.beside(result)
            operand = self.before(operand)
            self.advance()
        return operand


def sds(shape, dtype):
    return jax.ShapeDtypeStruct(shape, dtype)


def local(
    frames,
    lengths,
    norm_gain,
    norm_bias,
    qkv_weight,
    qv_bias,
    out_weight,
    out_bias,
    up_weight,
    up_bias,
    down_weight,
    down_bias,
    cotangent,
):
    micro, utts, t, _ = frames.shape
    rows = micro * utts
    segments = t // SEG
    sp = -(-segments // 16) * 16
    groups = t // GQ
    ext = HL + t + HR
    own_keys = ext - OWN0
    ff = up_weight.shape[1]
    tokens = rows * t
    total = t * lax.axis_size("tm")
    x = frames.reshape(rows, t, D)
    c = cotangent.reshape(rows, t, D)
    ob = out_bias.reshape(1, D)
    ub = up_bias.reshape(1, ff)
    db = down_bias.reshape(1, D)
    exchange = Exchange()
    steps = len(exchange.steps)
    bit = exchange.digits[0].reshape(1)

    pool = np.zeros((sp, t), np.float32)
    for s in range(segments):
        pool[s, s * SEG : (s + 1) * SEG] = 1
    poolh = np.zeros((16, HL), np.float32)
    for s in range(HL // SEG):
        poolh[16 - HL // SEG + s, s * SEG : (s + 1) * SEG] = 1
    expand = np.zeros((groups * MEMK, 16 + sp), np.float32)
    fold = np.zeros((sp, groups * MEMK), np.float32)
    for g in range(groups):
        for j in range(2 * MEMS - 1):
            seg = GROUP * g - MEMS + j
            expand[g * MEMK + j, 16 + seg] = 1
            if seg >= 0:
                fold[seg, g * MEMK + j] = 1
    place = np.zeros((sp, 16), np.float32)
    for j in range(MEMS):
        place[segments - MEMS + j, j] = 1
    hm8 = (np.arange(D)[None, :] // HD == np.arange(HEADS)[:, None]).astype(np.float32)
    hm4 = np.zeros((8, 256), np.float32)
    hm4[:4] = hm8[:4, :256]
    inside = np.zeros((KEYS, 128), np.float32)
    for lane in range(128):
        s = lane % GQ // SEG
        inside[s : s + MEMS, lane] = 1
        first = MEMK + 32 + s * SEG - LEFT
        inside[first : first + LEFT + SEG + RC, lane] = 1
    pool, poolh, expand, fold, place, hm8, hm4 = (
        jnp.asarray(v, bf16) for v in (pool, poolh, expand, fold, place, hm8, hm4)
    )
    inside = jnp.asarray(inside)

    pieces = []
    hop, need = 1, HL
    while need > 0:
        take = min(t, need)
        pieces.insert(0, shifted(x[:, t - take :], "tm", hop))
        need -= take
        hop += 1
    xl = jnp.concatenate(pieces, 1)
    xr = shifted(x[:, :HR], "tm", -1)

    q, k, v, nt, ns, pooled, pq = pl.pallas_call(
        own_kernel,
        grid=(rows,),
        in_specs=[
            row_spec((t, D)),
            const_spec((2, D)),
            const_spec((2, D)),
            const_spec((D, 3 * D)),
            const_spec((2, D)),
            const_spec((sp, t)),
        ],
        out_specs=[
            row_spec((t, D)),
            row_spec((ext, D)),
            row_spec((ext, D)),
            row_spec((D, t)),
            row_spec((sp, D)),
            row_spec((sp, D)),
            row_spec((sp, D)),
        ],
        out_shape=[
            sds((rows, t, D), bf16),
            sds((rows, ext, D), bf16),
            sds((rows, ext, D), bf16),
            sds((rows, D, t), bf16),
            sds((rows, sp, D), f32),
            sds((rows, sp, D), bf16),
            sds((rows, sp, D), bf16),
        ],
        scratch_shapes=[pltpu.VMEM((t, D), bf16), pltpu.VMEM((t, D), bf16)],
        compiler_params=params(),
        cost_estimate=cost(),
        name="own",
    )(x, norm_gain, norm_bias, qkv_weight, qv_bias, pool)

    any_spec = pl.BlockSpec(memory_space=pl.ANY)
    after_first = lambda r: (jnp.maximum(r - 1, 0), 0, 0)
    kext, vext, mkg, mvg, summary, memory, ps, p, attended = pl.pallas_call(
        functools.partial(memory_kernel, groups, total, utts),
        grid=(1 + rows,),
        in_specs=[
            smem_spec(),
            const_spec((rows, HL, D)),
            const_spec((rows, HR, D)),
            const_spec((rows, sp, D)),
            const_spec((2, D)),
            const_spec((2, D)),
            const_spec((D, 3 * D)),
            const_spec((2, D)),
            const_spec((D, D)),
            const_spec((1, D)),
            const_spec((16, HL)),
            const_spec((groups * MEMK, 16 + sp)),
            const_spec((HEADS, D)),
            any_spec,
            any_spec,
            pl.BlockSpec((1, t, D), after_first),
            const_spec((8, 256)),
            const_spec((KEYS, 128)),
        ],
        out_specs=[any_spec] * 7
        + [
            pl.BlockSpec((1, groups, KEYS, HEADS * GQ), lambda r: (jnp.maximum(r - 1, 0), 0, 0, 0)),
            pl.BlockSpec((1, t, D), after_first),
        ],
        out_shape=[
            sds((rows, ext, D), bf16),
            sds((rows, ext, D), bf16),
            sds((rows, groups * MEMK, D), bf16),
            sds((rows, groups * MEMK, D), bf16),
            sds((rows, sp, D), bf16),
            sds((rows, sp, D), bf16),
            sds((rows, own_keys, HEADS * sp), bf16),
            sds((rows, groups, KEYS, HEADS * GQ), bf16),
            sds((rows, t, D), bf16),
        ],
        scratch_shapes=[
            pltpu.VMEM((rows, ext, D), bf16),
            pltpu.VMEM((rows, ext, D), bf16),
            pltpu.VMEM((4, max(own_keys, HALO), HEADS * sp), f32),
            pltpu.VMEM((4, max(own_keys, HALO), HEADS * sp), bf16),
            pltpu.VMEM((rows, groups * MEMK, D), bf16),
            pltpu.VMEM((rows, groups * MEMK, D), bf16),
            pltpu.VMEM((rows, sp, D), bf16),
            pltpu.VMEM((rows, sp, D), bf16),
            pltpu.VMEM((rows, own_keys, HEADS * sp), bf16),
            pltpu.SemaphoreType.DMA((2,)),
            pltpu.SemaphoreType.DMA((4,)),
            pltpu.SemaphoreType.DMA((5,)),
        ],
        input_output_aliases={13: 0, 14: 1},
        compiler_params=params(),
        cost_estimate=cost(),
        name="attend",
    )(
        lengths,
        xl,
        xr,
        pq,
        norm_gain,
        norm_bias,
        qkv_weight,
        qv_bias,
        out_weight,
        ob,
        poolh,
        expand,
        hm8,
        k,
        v,
        q,
        hm4,
        inside,
    )

    tb = min(512, tokens)
    tiles = 8
    wide = ff // tiles
    token_spec = pl.BlockSpec((tb, D), lambda i: (i, 0))
    out, gmix, gatt, ff_keep, ff_send, outg, vec, upb = pl.pallas_call(
        functools.partial(ff_kernel, tiles),
        grid=(tokens // tb,),
        in_specs=[
            smem_spec(),
            token_spec,
            token_spec,
            token_spec,
            const_spec((2, D)),
            const_spec((2, D)),
            const_spec((D, D)),
            const_spec((1, D)),
            const_spec((D, ff)),
            const_spec((1, ff)),
            const_spec((ff, D)),
            const_spec((1, D)),
        ],
        out_specs=[
            token_spec,
            token_spec,
            token_spec,
            const_spec((D // 2, 2 * ff)),
            const_spec((D // 2, 2 * ff)),
            const_spec((D, D)),
            const_spec((8, D)),
            const_spec((1, ff)),
        ],
        out_shape=[
            sds((tokens, D), bf16),
            sds((tokens, D), bf16),
            sds((tokens, D), bf16),
            sds((D // 2, 2 * ff), bf16),
            sds((D // 2, 2 * ff), bf16),
            sds((D, D), f32),
            sds((8, D), f32),
            sds((1, ff), f32),
        ],
        scratch_shapes=[
            pltpu.VMEM((tb, D), f32),
            pltpu.VMEM((tb, 128), f32),
            pltpu.VMEM((tb, D), bf16),
            pltpu.VMEM((D + 16, tb), bf16),
            pltpu.VMEM((D, tb), bf16),
            pltpu.VMEM((tb, wide), f32),
            pltpu.VMEM((tb, wide), f32),
            pltpu.VMEM((tb, wide), bf16),
            pltpu.VMEM((tb, wide), bf16),
            pltpu.VMEM((tb, 2 * wide), bf16),
            pltpu.VMEM((tb, 2 * wide), bf16),
            pltpu.VMEM((tb, 2 * wide), bf16),
            pltpu.VMEM((tb, 2 * wide), bf16),
            pltpu.VMEM((tb, D), f32),
            pltpu.VMEM((tb, D), f32),
            pltpu.VMEM((D, ff), f32),
            pltpu.VMEM((D, ff), f32),
        ],
        compiler_params=params(),
        cost_estimate=cost(),
        name="feed_forward",
    )(
        bit,
        x.reshape(tokens, D),
        c.reshape(tokens, D),
        attended.reshape(tokens, D),
        norm_gain,
        norm_bias,
        out_weight,
        ob,
        up_weight,
        ub,
        down_weight,
        db,
    )
    gatt = gatt.reshape(rows, t, D)

    ff_sum = Running(exchange, ff_keep, ff_send)

    cut = groups * 3 // 8
    parts = [(0, cut), (cut, groups)] if cut else [(0, groups)]
    dqs, dks, dvs, dms = [], [], [], []
    for g0, g1 in parts:
        near = (g1 - g0) * GQ + NEAR - GQ
        if g0:
            gatt = ff_sum.along(dq, gatt)
        held = groups // 2 if g1 <= groups // 2 else groups
        dq, dk, dv, dm, first = pl.pallas_call(
            functools.partial(attend_back_kernel, g0, g1),
            grid=(rows,),
            in_specs=[
                row_spec((held * GQ, D)),
                row_spec((ext, D)),
                row_spec((ext, D)),
                row_spec((groups * MEMK, D)),
                row_spec((groups * MEMK, D)),
                row_spec((held, KEYS, HEADS * GQ)),
                row_spec((held * GQ, D)),
                const_spec((8, 256)),
            ],
            out_specs=[
                row_spec(((g1 - g0) * GQ, D)),
                row_spec((near, D)),
                row_spec((near, D)),
                row_spec(((g1 - g0) * MEMK, 2 * D)),
                row_spec((MEMK, 2 * D)),
            ],
            out_shape=[
                sds((rows, (g1 - g0) * GQ, D), bf16),
                sds((rows, near, D), bf16),
                sds((rows, near, D), bf16),
                sds((rows, (g1 - g0) * MEMK, 2 * D), bf16),
                sds((rows, MEMK, 2 * D), bf16),
            ],
            scratch_shapes=[pltpu.VMEM((near, D), f32), pltpu.VMEM((near, D), f32)],
            compiler_params=params(),
            cost_estimate=cost(),
            name="attend_back",
        )(q, kext, vext, mkg, mvg, p, gatt, hm4)
        for group, value in zip((dqs, dks, dvs, dms), (dq, dk, dv, dm)):
            group.append(value)
        if g0 == 0:
            recv = shifted(first, "tm", -1)

    recv = ff_sum.along(dq, recv)
    dko, dvo, left, right, gpq, dm, gm = pl.pallas_call(
        functools.partial(memory_back_kernel, parts),
        grid=(1,),
        in_specs=[const_spec(v.shape) for v in dms]
        + [any_spec] * (2 * len(parts))
        + [
            const_spec((rows, MEMK, 2 * D)),
            const_spec((sp, groups * MEMK)),
            const_spec((sp, MEMK)),
            const_spec((D, 3 * D)),
            const_spec((D, D)),
            const_spec((HEADS, D)),
            const_spec((rows, sp, D)),
            any_spec,
            any_spec,
            any_spec,
        ],
        out_specs=[
            any_spec,
            any_spec,
            const_spec((rows, 32, 2 * D)),
            const_spec((rows, HR, 2 * D)),
            const_spec((rows, sp, D)),
            const_spec((rows, sp, 2 * D)),
            const_spec((rows, sp, D)),
        ],
        out_shape=[
            sds((rows, t, D), bf16),
            sds((rows, t, D), bf16),
            sds((rows, 32, 2 * D), bf16),
            sds((rows, HR, 2 * D), bf16),
            sds((rows, sp, D), bf16),
            sds((rows, sp, 2 * D), bf16),
            sds((rows, sp, D), bf16),
        ],
        scratch_shapes=[
            pltpu.VMEM((rows, own_keys, D), bf16),
            pltpu.VMEM((rows, own_keys, D), bf16),
            pltpu.VMEM((rows, own_keys, HEADS * sp), bf16),
            pltpu.VMEM((rows, own_keys, HEADS * sp), f32),
            pltpu.VMEM((rows, own_keys, HEADS * sp), bf16),
            pltpu.VMEM((rows, own_keys, D), f32),
            pltpu.VMEM((rows, own_keys, D), f32),
            pltpu.VMEM((rows, t, D), bf16),
            pltpu.VMEM((rows, t, D), bf16),
        ]
        + [pltpu.VMEM(v.shape, bf16) for v in dks + dvs]
        + [pltpu.SemaphoreType.DMA((rows, 3 + 2 * len(parts))), pltpu.SemaphoreType.DMA((rows, 2))],
        compiler_params=params(),
        cost_estimate=cost(),
        name="memory_back",
    )(*dms, *dks, *dvs, recv, fold, place, qkv_weight, out_weight, hm8, pq, kext, vext, ps)

    from_right = shifted(left, "tm", -1)
    from_left = shifted(right, "tm", 1)
    gpq = ff_sum.along(gpq, gpq)
    dq_specs = [row_spec(v.shape[1:]) for v in dqs]
    accq, sums = pl.pallas_call(
        functools.partial(query_weights_kernel, len(dqs)),
        grid=(rows,),
        in_specs=[row_spec((D, t)), row_spec((sp, D))] + dq_specs + [row_spec((sp, D)), const_spec((D, D))],
        out_specs=[const_spec((D, D)), const_spec((8, D))],
        out_shape=[sds((D, D), f32), sds((8, D), f32)],
        compiler_params=params(),
        cost_estimate=cost(),
        name="query_weights",
    )(nt, ns, *dqs, gpq, qkv_weight)

    sums = ff_sum.along(sums, sums)
    keep, send = pl.pallas_call(
        key_weights_kernel,
        grid=(rows,),
        in_specs=[
            row_spec((D, t)),
            row_spec((t, D)),
            row_spec((t, D)),
            row_spec((32, 2 * D)),
            row_spec((HR, 2 * D)),
            const_spec((2, D)),
            const_spec((2, D)),
            const_spec((8, D)),
            const_spec((rows * sp, D)),
            const_spec((rows * sp, D)),
            const_spec((rows * sp, D)),
            const_spec((rows * sp, 2 * D)),
            const_spec((rows * sp, D)),
            const_spec((rows * sp, D)),
            const_spec((8, D)),
            const_spec((1, ff)),
            any_spec,
            any_spec,
            any_spec,
            smem_spec(),
        ],
        out_specs=[pl.BlockSpec(memory_space=pltpu.VMEM)] * 2,
        out_shape=[in_vmem((D // 2, 4 * D + 128), bf16)] * 2,
        scratch_shapes=[
            pltpu.VMEM((D, 2 * D), f32),
            pltpu.VMEM((1, 2 * D), f32),
            pltpu.VMEM((D, D), f32),
            pltpu.VMEM((4, D, 128), f32),
            pltpu.VMEM((D, 3 * D), bf16),
            pltpu.VMEM((D, D), f32),
            pltpu.VMEM((D, D), f32),
            pltpu.SemaphoreType.DMA((3,)),
        ],
        compiler_params=params(56),
        cost_estimate=cost(),
        name="key_weights",
    )(
        nt,
        dko,
        dvo,
        from_right,
        from_left,
        norm_gain,
        norm_bias,
        sums,
        pooled.reshape(rows * sp, D),
        gpq.reshape(rows * sp, D),
        memory.reshape(rows * sp, D),
        dm.reshape(rows * sp, 2 * D),
        summary.reshape(rows * sp, D),
        gm.reshape(rows * sp, D),
        vec,
        upb,
        qkv_weight,
        accq,
        outg,
        bit,
    )
    ff_sum.beside(send)
    send = ff_sum.before(send)
    rest = Running(exchange, keep, send)
    gpq = rest.before(gpq)
    fg = pl.pallas_call(
        functools.partial(own_frames_kernel, len(dqs)),
        grid=(rows,),
        in_specs=[row_spec((t, D))]
        + dq_specs
        + [
            row_spec((t, D)),
            row_spec((t, D)),
            row_spec((32, 2 * D)),
            row_spec((HR, 2 * D)),
            row_spec((sp, D)),
            row_spec((t, D)),
            const_spec((2, D)),
            const_spec((D, 3 * D)),
        ],
        out_specs=row_spec((t, D)),
        out_shape=sds((rows, t, D), bf16),
        scratch_shapes=[pltpu.VMEM((t, D), f32)],
        compiler_params=params(56),
        cost_estimate=cost(),
        name="own_frames",
    )(x, *dqs, dko, dvo, from_right, from_left, gpq, gmix.reshape(rows, t, D), norm_gain, qkv_weight)
    turns = [steps - 2, steps - 1, steps + 1] if ff_sum.last - ff_sum.phase <= 3 else list(range(1, 2 * steps - 1))
    while rest.phase < rest.last:
        if rest.phase == 1:
            rest.beside(fg)
        if rest.phase in turns and ff_sum.phase < ff_sum.last:
            ff_sum.arriving, rest.arriving = lax.optimization_barrier((ff_sum.arriving, rest.arriving))
            ff_sum.advance()
        if rest.phase == rest.last - 1:
            blocks = ff // D
            half = D // 2
            up_sum, down_sum = pl.pallas_call(
                unpack_ff_kernel,
                grid=(blocks,),
                in_specs=[smem_spec()]
                + [pl.BlockSpec((half, D), lambda i: (0, i))] * 2
                + [pl.BlockSpec((half, D), lambda i: (0, i + blocks))] * 2,
                out_specs=[pl.BlockSpec((D, D), lambda i: (0, i)), pl.BlockSpec((D, D), lambda i: (i, 0))],
                out_shape=[sds((D, ff), f32), sds((ff, D), f32)],
                compiler_params=params(28),
                cost_estimate=cost(),
                name="unpack_feed_forward",
            )(bit, ff_sum.value, ff_sum.arriving[0], ff_sum.value, ff_sum.arriving[0])
            rest.beside(up_sum)
        rest.advance()
    grads, other = rest.value, rest.arriving[0]
    half = D // 2
    part_spec = pl.BlockSpec((half, D), lambda i, side: (0, i))
    vector_spec = pl.BlockSpec((half, 128), lambda i, side: (0, 4 * D // 128), pipeline_mode=pl.Buffered(1))
    big_specs = [
        pl.BlockSpec((half, D), lambda i, side: (side[0], jnp.minimum(i, 2))),
        pl.BlockSpec((half, D), lambda i, side: (side[0], 0)),
    ]
    big_shapes = [sds((D, 3 * D), f32), sds((D, D), f32)]
    qkv_sum, out_sum = pl.pallas_call(
        unpack_own_kernel,
        grid_spec=pltpu.PrefetchScalarGridSpec(
            num_scalar_prefetch=1, grid=(4,), in_specs=[part_spec], out_specs=big_specs
        ),
        out_shape=big_shapes,
        compiler_params=params(28),
        cost_estimate=cost(),
        name="unpack_own",
    )(bit, grads)
    small_shapes = [(2, D), (2, D), (2, D), (1, D), (1, ff), (1, D)]
    other, qkv_sum = lax.optimization_barrier((other, qkv_sum))
    qkv_sum, out_sum, gain_sum, bias_sum, qvb_sum, outb_sum, upb_sum, downb_sum = pl.pallas_call(
        unpack_rest_kernel,
        grid_spec=pltpu.PrefetchScalarGridSpec(
            num_scalar_prefetch=1,
            grid=(4,),
            in_specs=[part_spec, vector_spec, vector_spec, any_spec, any_spec],
            out_specs=big_specs
            + [pl.BlockSpec(v, lambda i, side: (0, 0), pipeline_mode=pl.Buffered(1)) for v in small_shapes],
        ),
        out_shape=big_shapes + [sds(v, f32) for v in small_shapes],
        input_output_aliases={4: 0, 5: 1},
        compiler_params=params(28),
        cost_estimate=cost(),
        name="unpack_rest",
    )(1 - bit, other, grads, other, qkv_sum, out_sum)
    return (
        out.reshape(micro, utts, t, D),
        fg.reshape(micro, utts, t, D),
        gain_sum,
        bias_sum,
        qkv_sum,
        qvb_sum,
        out_sum,
        outb_sum.reshape(D),
        up_sum,
        upb_sum.reshape(ff),
        down_sum,
        downb_sum.reshape(D),
    )


def solution(mesh):
    spread = P(None, "dp", "tm", None)
    in_specs = (spread, P("dp")) + (P(),) * 10 + (spread,)
    out_specs = (spread, spread) + (P(),) * 10
    return jax.shard_map(local, mesh=mesh, in_specs=in_specs, out_specs=out_specs, check_vma=False)
```

```python
import functools

import jax
import jax.numpy as jnp
import numpy as np
from jax import lax
from jax.experimental import pallas as pl
from jax.experimental.pallas import tpu as pltpu
from jax.sharding import PartitionSpec as P

HEADS = 8
SEG = 16
LEFT = 30
RC = 4
MEMS = 4
D = 512
HD = D // HEADS
GROUP = 4
GQ = GROUP * SEG
NEAR = 112
MEMK = 16
KEYS = MEMK + NEAR
HL = 96
HR = 16
HALO = HL + HR
OWN0 = HL - 32
SCALE = HD**-0.5
NEG = -1000000000.0
MB = 1024 * 1024

f32 = jnp.float32
bf16 = jnp.bfloat16


def dot(a, b):
    return lax.dot_general(a, b, (((1,), (0,)), ((), ())), preferred_element_type=f32)


def dot_nt(a, b):
    return lax.dot_general(a, b, (((1,), (1,)), ((), ())), preferred_element_type=f32)


def dot_tn(a, b):
    return lax.dot_general(a, b, (((0,), (0,)), ((), ())), preferred_element_type=f32)


def normalize(x):
    center = x - jnp.mean(x, axis=-1, keepdims=True)
    spread = jnp.mean(center * center, axis=-1, keepdims=True)
    r = lax.rsqrt(spread + 1e-05)
    return center * r, r


def norm_back(grad_y, n, r, gain):
    d = grad_y * gain
    return r * (d - jnp.mean(d, axis=-1, keepdims=True) - n * jnp.mean(d * n, axis=-1, keepdims=True))


def col_sum(v):
    return jnp.sum(v, axis=0, keepdims=True)


def row_blocks(rows, most):
    size = max(d for d in range(16, most + 1, 16) if rows % d == 0)
    return [slice(r0, r0 + size) for r0 in range(0, rows, size)]


def fold_rows(v, op=jnp.sum):
    return op(v.reshape(-1, 8, v.shape[-1]), axis=0)


def block_diag(rows, masks):
    return jnp.concatenate([rows * m for m in masks], 0)


def pick_heads(r, rows):
    lane = lax.broadcasted_iota(jnp.int32, (rows, 128), 1)
    return jnp.where(lane < HD, r[:rows], r[rows:])


def valid_frames(f, total, length):
    return (f >= 0) & (f < total) & ((f < length) | ((f & (SEG - 1)) == 0))


def softmax_rows(s):
    m = jnp.max(s, axis=0, keepdims=True)
    e = jnp.exp(s - m)
    return e * (1.0 / jnp.sum(e, axis=0, keepdims=True))


def const_spec(shape):
    zeros = (0,) * len(shape)
    return pl.BlockSpec(shape, lambda r: zeros, pipeline_mode=pl.Buffered(1))


def row_spec(shape):
    zeros = (0,) * len(shape)
    return pl.BlockSpec((1,) + shape, lambda r: (r,) + zeros)


def in_vmem(shape, dtype):
    return pltpu.VMEM(shape, dtype)


def smem_spec():
    return pl.BlockSpec(memory_space=pltpu.SMEM)


def params(mb=60):
    return pltpu.CompilerParams(dimension_semantics=("arbitrary",), vmem_limit_bytes=mb * MB)


def cost():
    return pl.CostEstimate(flops=1000000, bytes_accessed=100000, transcendentals=0)


def own_kernel(
    x_ref,
    gain_ref,
    bias_ref,
    w_ref,
    qvb_ref,
    pool_ref,
    q_ref,
    k_ref,
    v_ref,
    nt_ref,
    ns_ref,
    pooled_ref,
    pq_ref,
    low_s,
    n_s,
):
    t = x_ref.shape[1]
    for rows in row_blocks(t, 32):
        n, _ = normalize(x_ref[0, rows].astype(f32))
        low_s[rows] = (n * gain_ref[0:1] + bias_ref[0:1]).astype(bf16)
        n_s[rows] = n.astype(bf16)
    low = low_s[...]
    q_ref[0] = ((dot(low, w_ref[:, :D]) + qvb_ref[0:1]) * SCALE).astype(bf16)
    for rows in row_blocks(t, 128):
        nt_ref[0, :, rows] = n_s[rows].T
    k_ref[0, HL : HL + t] = dot(low, w_ref[:, D : 2 * D]).astype(bf16)
    v_ref[0, HL : HL + t] = (dot(low, w_ref[:, 2 * D :]) + qvb_ref[1:2]).astype(bf16)
    ns_ref[0] = dot(pool_ref[...], n_s[...])
    pooled = (dot(pool_ref[...], low) * (1.0 / SEG)).astype(bf16)
    pooled_ref[0] = pooled
    pq_ref[0] = ((dot(pooled, w_ref[:, :D]) + qvb_ref[0:1]) * SCALE).astype(bf16)


def near_mask(keys, lanes, seg_mask, seg0, frame0, position, total, length):
    f = lax.broadcasted_iota(jnp.int32, (keys, lanes), 0) + frame0
    seg = (lax.broadcasted_iota(jnp.int32, (keys, lanes), 1) & seg_mask) + seg0
    start = seg * SEG
    ok = (f >= start - LEFT) & (f < start + (SEG + RC))
    return ok & valid_frames(f + position, total, length)


def memory_kernel(
    groups,
    total,
    utts,
    len_ref,
    xl_ref,
    xr_ref,
    pq_ref,
    gain_ref,
    bias_ref,
    w_ref,
    qvb_ref,
    ow_ref,
    ob_ref,
    poolh_ref,
    expand_ref,
    hm8_ref,
    kin_ref,
    vin_ref,
    q_ref,
    hm4_ref,
    inside_ref,
    kext_ref,
    vext_ref,
    mkg_hbm,
    mvg_hbm,
    summary_hbm,
    memory_hbm,
    ps_hbm,
    p_ref,
    att_ref,
    k_s,
    v_s,
    score_s,
    prob_s,
    mkg_ref,
    mvg_ref,
    summary_ref,
    memory_ref,
    ps_ref,
    in_sem,
    out_sem,
    early_sem,
):
    step = pl.program_id(0)
    early_refs = (mkg_hbm, mvg_hbm, summary_hbm, memory_hbm, ps_hbm)

    @pl.when(step == pl.num_programs(0) - 1)
    def _():
        for value, out, sem in zip((mkg_ref, mvg_ref, summary_ref, memory_ref, ps_ref), early_refs, range(5)):
            pltpu.make_async_copy(value, out, early_sem.at[sem]).wait()

    @pl.when(step == 0)
    def _():
        memory_step(
            total,
            utts,
            len_ref,
            xl_ref,
            xr_ref,
            pq_ref,
            gain_ref,
            bias_ref,
            w_ref,
            qvb_ref,
            ow_ref,
            ob_ref,
            poolh_ref,
            expand_ref,
            hm8_ref,
            kin_ref,
            vin_ref,
            kext_ref,
            vext_ref,
            mkg_ref,
            mvg_ref,
            summary_ref,
            memory_ref,
            ps_ref,
            k_s,
            v_s,
            score_s,
            prob_s,
            in_sem,
            out_sem,
            early_refs,
            early_sem,
        )

    @pl.when(step > 0)
    def _():
        row = step - 1
        attend_step(
            groups,
            total,
            len_ref[lax.rem(row, utts)],
            q_ref,
            k_s.at[pl.ds(row, 1)],
            v_s.at[pl.ds(row, 1)],
            mkg_ref.at[pl.ds(row, 1)],
            mvg_ref.at[pl.ds(row, 1)],
            hm4_ref,
            inside_ref,
            p_ref,
            att_ref,
        )


def memory_step(
    total,
    utts,
    len_ref,
    xl_ref,
    xr_ref,
    pq_ref,
    gain_ref,
    bias_ref,
    w_ref,
    qvb_ref,
    ow_ref,
    ob_ref,
    poolh_ref,
    expand_ref,
    hm8_ref,
    kin_ref,
    vin_ref,
    kext_ref,
    vext_ref,
    mkg_ref,
    mvg_ref,
    summary_ref,
    memory_ref,
    ps_ref,
    k_s,
    v_s,
    score_s,
    prob_s,
    in_sem,
    out_sem,
    early_refs,
    early_sem,
):
    rows, ext, _ = k_s.shape
    t = ext - HALO
    sp = pq_ref.shape[1]
    own_keys = ext - OWN0
    loads = [pltpu.make_async_copy(kin_ref, k_s, in_sem.at[0]), pltpu.make_async_copy(vin_ref, v_s, in_sem.at[1])]
    for load in loads:
        load.start()
    position = lax.axis_index("tm") * t
    halo = [xl_ref[...].reshape(rows * HL, D), xr_ref[...].reshape(rows * HR, D)]
    n, _ = normalize(jnp.concatenate(halo, 0).astype(f32))
    low = (n * gain_ref[0:1] + bias_ref[0:1]).astype(bf16)
    kh = dot(low, w_ref[:, D : 2 * D]).astype(bf16)
    vh = (dot(low, w_ref[:, 2 * D :]) + qvb_ref[1:2]).astype(bf16)
    pooled = [dot(poolh_ref[...], low[r * HL : (r + 1) * HL]) * (1.0 / SEG) for r in range(rows)]
    pooled = jnp.concatenate(pooled, 0).astype(bf16)
    pqh = ((dot(pooled, w_ref[:, :D]) + qvb_ref[0:1]) * SCALE).astype(bf16)
    for load in loads:
        load.wait()
    for scratch, value in ((k_s, kh), (v_s, vh)):
        for r in range(rows):
            scratch[r, :HL] = value[r * HL : (r + 1) * HL]
            scratch[r, HL + t :] = value[rows * HL + r * HR : rows * HL + (r + 1) * HR]
    stores = []
    for i, (scratch, out) in enumerate(((k_s, kext_ref), (v_s, vext_ref))):
        for j, part in enumerate((pl.ds(0, HL), pl.ds(HL + t, HR))):
            stores.append(pltpu.make_async_copy(scratch.at[:, part], out.at[:, part], out_sem.at[2 * i + j]))
    for store in stores:
        store.start()
    masks8 = [hm8_ref[h : h + 1] for h in range(HEADS)]
    jobs = []
    for r in range(rows):
        jobs.append((r, slice(0, HALO), 16, -16, -HL))
        jobs.append((r, slice(OWN0, ext), sp, 0, -32))
    sums = []
    for step in range(len(jobs) + 2):
        if step < len(jobs):
            r, keys, count, _, _ = jobs[step]
            pq = pqh[r * 16 : (r + 1) * 16] if step % 2 == 0 else pq_ref[r]
            score_s[step % 4, : keys.stop - keys.start, : HEADS * count] = dot_nt(k_s[r, keys], block_diag(pq, masks8))
        if 1 <= step <= len(jobs):
            r, keys, count, seg0, frame0 = jobs[step - 1]
            score, prob = score_s.at[(step - 1) % 4], prob_s.at[(step - 1) % 4]
            blocks = row_blocks(keys.stop - keys.start, 128)
            for l0 in range(0, HEADS * count, 128):
                lanes = slice(l0, l0 + 128)
                most = None
                for block in blocks:
                    shape = (block.stop - block.start, 128)
                    mask = near_mask(*shape, count - 1, seg0, frame0 + block.start, position, total, len_ref[r % utts])
                    value = jnp.where(mask, score[block, lanes], NEG)
                    score[block, lanes] = value
                    value = fold_rows(value, jnp.max)
                    most = value if most is None else jnp.maximum(most, value)
                most = jnp.max(most, axis=0, keepdims=True)
                weight = 0.0
                for block in blocks:
                    value = jnp.exp(score[block, lanes] - most)
                    score[block, lanes] = value
                    weight += fold_rows(value)
                weight = 1.0 / col_sum(weight)
                for block in blocks:
                    value = (score[block, lanes] * weight).astype(bf16)
                    prob[block, lanes] = value
                    if step % 2 == 0:
                        ps_ref[r, block, lanes] = value
        if step >= 2:
            r, keys, count, _, _ = jobs[step - 2]
            prob = prob_s[(step - 2) % 4, : keys.stop - keys.start, : HEADS * count]
            o = dot_tn(prob, v_s[r, keys])
            o = [
                pick_heads(o[2 * j * count : (2 * j + 2) * count, 128 * j : 128 * j + 128], count)
                for j in range(HEADS // 2)
            ]
            sums.append(jnp.concatenate(o, 1).astype(bf16))
            if step % 2:
                summary_ref[r] = sums[-1]
    memory = (dot(jnp.concatenate(sums, 0), ow_ref[...]) + ob_ref[...]).astype(bf16)
    mk = dot(memory, w_ref[:, D : 2 * D]).astype(bf16)
    mv = (dot(memory, w_ref[:, 2 * D :]) + qvb_ref[1:2]).astype(bf16)
    for r in range(rows):
        here = slice(r * (16 + sp), (r + 1) * (16 + sp))
        memory_ref[r] = memory[here][16:]
        mkg_ref[r] = dot(expand_ref[...], mk[here]).astype(bf16)
        mvg_ref[r] = dot(expand_ref[...], mv[here]).astype(bf16)
    for value, out, sem in zip((mkg_ref, mvg_ref, summary_ref, memory_ref, ps_ref), early_refs, range(5)):
        pltpu.make_async_copy(value, out, early_sem.at[sem]).start()
    for store in stores:
        store.wait()


def group_keys(ref, mem_ref, g):
    k0 = g * GQ + OWN0
    return jnp.concatenate([mem_ref[0, g * MEMK : (g + 1) * MEMK], ref[0, k0 : k0 + NEAR]], 0)


def attend_step(
    groups, total, length, q_ref, kext_ref, vext_ref, mkg_ref, mvg_ref, hm4_ref, inside_ref, p_ref, att_ref
):
    position = lax.axis_index("tm") * q_ref.shape[1]
    masks4 = [hm4_ref[h : h + 1] for h in range(4)]
    slot = lax.broadcasted_iota(jnp.int32, (KEYS, 128), 0)
    inside = inside_ref[...] > 0.5
    scores, probs = {}, {}
    for step in range(groups + 2):
        if step < groups:
            g = step
            q = q_ref[0, g * GQ : (g + 1) * GQ]
            kc = group_keys(kext_ref, mkg_ref, g)
            for quad in range(2):
                c0 = 256 * quad
                scores[g, quad] = dot_nt(kc[:, c0 : c0 + 256], block_diag(q[:, c0 : c0 + 256], masks4))
        if 1 <= step <= groups:
            g = step - 1
            f = jnp.where(slot < MEMK, (slot + (g * GROUP - MEMS)) * SEG, slot + (g * GQ - 32 - MEMK)) + position
            keep = inside & valid_frames(f, total, length)
            for pair in range(HEADS // 2):
                cp = 128 * pair
                s = scores[g, pair // 2][:, 128 * (pair % 2) : 128 * (pair % 2) + 128]
                probs[g, pair] = softmax_rows(jnp.where(keep, s, NEG)).astype(bf16)
                p_ref[0, g, :, cp : cp + 128] = probs[g, pair]
        if step >= 2:
            g = step - 2
            vc = group_keys(vext_ref, mvg_ref, g)
            for pair in range(HEADS // 2):
                cp = 128 * pair
                r = dot_tn(probs[g, pair], vc[:, cp : cp + 128])
                att_ref[0, g * GQ : (g + 1) * GQ, cp : cp + 128] = pick_heads(r, GQ).astype(bf16)


def split_halves(bit_ref, keep_ref, send_ref, cols, src_ref):
    half = D // 2

    @pl.when(bit_ref[0] == 0)
    def _():
        keep_ref[:, cols] = src_ref[:half].astype(bf16)
        send_ref[:, cols] = src_ref[half:].astype(bf16)

    @pl.when(bit_ref[0] != 0)
    def _():
        keep_ref[:, cols] = src_ref[half:].astype(bf16)
        send_ref[:, cols] = src_ref[:half].astype(bf16)


def gelu_both(v):
    e = jnp.exp2(v * v * (-0.5 * 1.4426950408889634))
    t = pl.reciprocal(1.0 + jnp.abs(v) * (0.3275911 * 0.5**0.5), approx=True)
    e, t, v = e.astype(bf16), t.astype(bf16), v.astype(bf16)
    poly = 0.5 * -1.453152027 + t * (0.5 * 1.061405429)
    poly = 0.5 * 1.421413741 + t * poly
    poly = 0.5 * -0.284496736 + t * poly
    poly = 0.5 * 0.254829592 + t * poly
    tail = t * poly * e
    phi = jnp.where(v >= 0, 1 - tail, tail)
    return v * phi, phi + v * (e * 0.3989422804014327)


def ff_kernel(
    tiles,
    bit_ref,
    x_ref,
    c_ref,
    att_ref,
    gain_ref,
    bias_ref,
    ow_ref,
    ob_ref,
    uw_ref,
    ub_ref,
    dw_ref,
    db_ref,
    out_ref,
    gmix_ref,
    gatt_ref,
    keep_ref,
    send_ref,
    outg_ref,
    vec_ref,
    upb_ref,
    n_s,
    r_s,
    n2_s,
    n2t_s,
    ct_s,
    up0_s,
    up1_s,
    da0_s,
    da1_s,
    act0_s,
    act1_s,
    dup0_s,
    dup1_s,
    acc_s,
    gy_s,
    upg_s,
    dng_s,
):
    step = pl.program_id(0)
    ff = uw_ref.shape[1]
    wide = ff // tiles
    up_s, da_s, act_s, dup_s = (up0_s, up1_s), (da0_s, da1_s), (act0_s, act1_s), (dup0_s, dup1_s)

    @pl.when(step == 0)
    def _():
        upg_s[...] = jnp.zeros_like(upg_s)
        dng_s[...] = jnp.zeros_like(dng_s)
        outg_ref[...] = jnp.zeros_like(outg_ref)
        vec_ref[...] = jnp.zeros_like(vec_ref)
        upb_ref[...] = jnp.zeros_like(upb_ref)

    gy_s[...] = x_ref[...].astype(f32) + dot(att_ref[...], ow_ref[...]) + ob_ref[...]
    for rows in row_blocks(x_ref.shape[0], 32):
        mixed = gy_s[rows]
        n, r = normalize(mixed)
        n_s[rows] = n
        r_s[rows] = jnp.broadcast_to(r, (mixed.shape[0], 128))
        n2_s[rows] = (n * gain_ref[1:2] + bias_ref[1:2]).astype(bf16)
        acc_s[rows] = mixed + db_ref[...]
    for rows in row_blocks(x_ref.shape[0], 128):
        n2t_s[:D, rows] = n2_s[rows].T
        ct_s[:, rows] = c_ref[rows].T
    n2t_s[D:] = jnp.ones((16, x_ref.shape[0]), bf16)

    tb = x_ref.shape[0]
    chunk = min(256, tb)

    def gelu_rows(i, few):
        half = slice((i % 2) * wide, (i % 2 + 1) * wide)
        act, slope = gelu_both(up_s[i % 2][few])
        act_s[i // 2 % 2][few, half] = act
        dup_s[i // 2 % 2][few, half] = slope * da_s[i % 2][few]

    for j in range(tiles + 2):
        pieces = row_blocks(tb, 64) if 1 <= j <= tiles else []

        def some(count):
            for few in pieces[:count]:
                gelu_rows(j - 1, few)
            del pieces[:count]

        for r0 in range(0, tb, chunk):
            rows = slice(r0, r0 + chunk)
            some(2)
            if j < tiles:
                cols = slice(j * wide, (j + 1) * wide)
                up_s[j % 2][rows] = dot(n2_s[rows], uw_ref[:, cols]) + ub_ref[:, cols]
                some(1)
                da_s[j % 2][rows] = dot_nt(c_ref[rows], dw_ref[cols, :]).astype(bf16)
            some(1)
            if j >= 2 and j % 2:
                i = j - 2
                both = slice((i - 1) * wide, (i + 1) * wide)
                acc_s[rows] += dot(act_s[i // 2 % 2][rows], dw_ref[both, :])
                back = dot_nt(dup_s[i // 2 % 2][rows], uw_ref[:, both])
                gy_s[rows] = back if i == 1 else gy_s[rows] + back
        some(len(pieces))
        if j >= 2:
            i = j - 2
            cols = slice(i * wide, (i + 1) * wide)
            half = slice((i % 2) * wide, (i % 2 + 1) * wide)
            grad = dot(n2t_s[...], dup_s[i // 2 % 2][:, half])
            upg_s[:, cols] += grad[:D]
            upb_ref[:, cols] += grad[D : D + 1]
            dng_s[:, cols] += dot(ct_s[...], act_s[i // 2 % 2][:, half])

    sums = [0.0] * 4
    for rows in row_blocks(x_ref.shape[0], 32):
        out_ref[rows] = acc_s[rows].astype(bf16)
        n = n_s[rows]
        cf = c_ref[rows].astype(f32)
        gy = gy_s[rows]
        gmix = cf + norm_back(gy, n, r_s[rows, 0:1], gain_ref[1:2])
        gmix_ref[rows] = gmix.astype(bf16)
        sums = [a + fold_rows(b) for a, b in zip(sums, (gy * n, gy, gmix, cf))]
    branch = gmix_ref[...]
    gatt_ref[...] = dot_nt(branch, ow_ref[...]).astype(bf16)
    outg_ref[...] += dot_tn(att_ref[...], branch)
    for i, value in enumerate(sums):
        vec_ref[i : i + 1] += col_sum(value)

    @pl.when(step == pl.num_programs(0) - 1)
    def _():
        split_halves(bit_ref, keep_ref, send_ref, slice(0, ff), upg_s)
        split_halves(bit_ref, keep_ref, send_ref, slice(ff, 2 * ff), dng_s)


def attend_back_kernel(
    g0,
    g1,
    q_ref,
    kext_ref,
    vext_ref,
    mkg_ref,
    mvg_ref,
    p_ref,
    g_ref,
    hm4_ref,
    dq_ref,
    dk_ref,
    dv_ref,
    dm_ref,
    first_ref,
    dk_s,
    dv_s,
):
    dk_s[...] = jnp.zeros_like(dk_s)
    dv_s[...] = jnp.zeros_like(dv_s)
    masks4 = [hm4_ref[h : h + 1] for h in range(4)]
    count = g1 - g0
    grads, backs = {}, {}
    for step in range(count + 2):
        if step < count:
            g = step
            go = g_ref[0, (g0 + g) * GQ : (g0 + g + 1) * GQ]
            vc = group_keys(vext_ref, mvg_ref, g0 + g)
            for quad in range(2):
                cols = slice(256 * quad, 256 * quad + 256)
                grads[g, quad] = dot_nt(vc[:, cols], block_diag(go[:, cols], masks4))
        if 1 <= step <= count:
            g = step - 1
            for pair in range(HEADS // 2):
                half = slice(128 * (pair % 2), 128 * (pair % 2) + 128)
                p = p_ref[0, g0 + g, :, 128 * pair : 128 * pair + 128].astype(f32)
                pdp = p * grads[g, pair // 2][:, half]
                backs[g, pair] = (pdp - p * col_sum(pdp)).astype(bf16)
        if step >= 2:
            g = step - 2
            here = slice(g * GQ, (g + 1) * GQ)
            near = slice(g * GQ, g * GQ + NEAR)
            mem = slice(g * MEMK, (g + 1) * MEMK)
            there = slice((g0 + g) * GQ, (g0 + g + 1) * GQ)
            q = q_ref[0, there]
            go = g_ref[0, there]
            kc = group_keys(kext_ref, mkg_ref, g0 + g)
            for quad in range(2):
                c0 = 256 * quad
                cols = slice(c0, c0 + 256)
                dv_cols = slice(D + c0, D + c0 + 256)
                ds = jnp.concatenate([backs[g, 2 * quad], backs[g, 2 * quad + 1]], 1)
                dv = dot(p_ref[0, g0 + g, :, cols], block_diag(go[:, cols], masks4))
                dk = dot(ds, block_diag(q[:, cols], masks4))
                dm_ref[0, mem, cols] = dk[:MEMK].astype(bf16)
                dm_ref[0, mem, dv_cols] = dv[:MEMK].astype(bf16)
                if g0 + g == 0:
                    first_ref[0, :, cols] = dk[:MEMK].astype(bf16)
                    first_ref[0, :, dv_cols] = dv[:MEMK].astype(bf16)
                dk_s[near, cols] += dk[MEMK:]
                dv_s[near, cols] += dv[MEMK:]
                for pair in range(2):
                    cp = c0 + 128 * pair
                    r = dot_tn(backs[g, 2 * quad + pair], kc[:, cp : cp + 128])
                    dq_ref[0, here, cp : cp + 128] = (pick_heads(r, GQ) * SCALE).astype(bf16)
    dk_ref[0] = dk_s[...].astype(bf16)
    dv_ref[0] = dv_s[...].astype(bf16)
    if g0:
        first_ref[...] = jnp.zeros_like(first_ref)


def memory_back_kernel(parts, *refs):
    count = len(parts)
    dm_refs, main_hbm = refs[:count], refs[count : 3 * count]
    (
        recv_ref,
        fold_ref,
        place_ref,
        w_ref,
        ow_ref,
        hm8_ref,
        pq_ref,
        kext_hbm,
        vext_hbm,
        ps_hbm,
        dko_hbm,
        dvo_hbm,
        left_ref,
        right_ref,
        gpq_ref,
        dmo_ref,
        gm_ref,
        k_s,
        v_s,
        ps_s,
        dp_s,
        ds_s,
        dk_s,
        dv_s,
        dko_s,
        dvo_s,
        *main_s,
        in_sems,
        out_sems,
    ) = refs[3 * count :]
    rows, sp, _ = pq_ref.shape
    t = dko_s.shape[1]
    own = pl.ds(OWN0, k_s.shape[1])
    loads = []
    for r in range(rows):
        pairs = [(vext_hbm.at[r, own], v_s.at[r]), (ps_hbm.at[r], ps_s.at[r]), (kext_hbm.at[r, own], k_s.at[r])]
        pairs += [(src.at[r], held.at[r]) for src, held in zip(main_hbm, main_s)]
        loads.append([pltpu.make_async_copy(src, dst, in_sems.at[r, i]) for i, (src, dst) in enumerate(pairs)])
    for row in loads:
        for load in row:
            load.start()
    stores = []
    for r in range(rows):
        pairs = ((dko_s.at[r], dko_hbm.at[r]), (dvo_s.at[r], dvo_hbm.at[r]))
        stores.append([pltpu.make_async_copy(src, dst, out_sems.at[r, i]) for i, (src, dst) in enumerate(pairs)])
    masks8 = [hm8_ref[h : h + 1] for h in range(HEADS)]

    def fold(r):
        got = dot(fold_ref[...], jnp.concatenate([ref[r] for ref in dm_refs], 0))
        return (got + dot(place_ref[...], recv_ref[r])).astype(bf16)

    dm = jnp.concatenate([fold(r) for r in range(rows)], 0)
    gm = dot_nt(dm, w_ref[:, D:]).astype(bf16)
    gs = dot_nt(gm, ow_ref[...]).astype(bf16)
    for r in range(rows):
        dmo_ref[r] = dm[r * sp : (r + 1) * sp]
        gm_ref[r] = gm[r * sp : (r + 1) * sp]
    gbd = {}
    blocks = row_blocks(dp_s.shape[1], 128)
    for step in range(rows + 2):
        if step < rows:
            loads[step][0].wait()
        if 1 <= step <= rows:
            loads[step - 1][1].wait()
        if step >= 2:
            for load in loads[step - 2][2:]:
                load.wait()
        if step < rows:
            r = step
            gbd[r] = block_diag(gs[r * sp : (r + 1) * sp], masks8)
            dp_s[r] = dot_nt(v_s[r], gbd[r])
        if 1 <= step <= rows:
            r = step - 1
            for l0 in range(0, HEADS * sp, 128):
                lanes = slice(l0, l0 + 128)
                weight = 0.0
                for block in blocks:
                    pdp = ps_s[r, block, lanes].astype(f32) * dp_s[r, block, lanes]
                    dp_s[r, block, lanes] = pdp
                    weight += fold_rows(pdp)
                weight = col_sum(weight)
                for block in blocks:
                    p = ps_s[r, block, lanes].astype(f32)
                    ds_s[r, block, lanes] = (dp_s[r, block, lanes] - p * weight).astype(bf16)
        if step >= 2:
            r = step - 2
            ds = ds_s[r]
            dq = dot_tn(ds, k_s[r])
            dq = [
                pick_heads(dq[2 * j * sp : (2 * j + 2) * sp, 128 * j : 128 * j + 128], sp)
                for j in range(HEADS // 2)
            ]
            gpq_ref[r] = (jnp.concatenate(dq, 1) * SCALE).astype(bf16)
            for left, right, sum_s, held, out_s, cols in (
                (ds, block_diag(pq_ref[r], masks8), dk_s, main_s[:count], dko_s, slice(0, D)),
                (ps_s[r], gbd[r], dv_s, main_s[count:], dvo_s, slice(D, 2 * D)),
            ):
                sum_s[r] = dot(left, right)
                for (g0, _), main in zip(parts, held):
                    sum_s[r, g0 * GQ : g0 * GQ + main.shape[1]] += main[r].astype(f32)
                left_ref[r, :, cols] = sum_s[r, :32].astype(bf16)
                out_s[r] = sum_s[r, 32 : 32 + t].astype(bf16)
                right_ref[r, :, cols] = sum_s[r, 32 + t :].astype(bf16)
            for store in stores[r]:
                store.start()
    for row in stores:
        for store in row:
            store.wait()


def query_weights_kernel(count, nt_ref, ns_ref, *refs):
    dq_refs = refs[:count]
    gpq_ref, w_ref, acc_ref, sum_ref = refs[count:]

    @pl.when(pl.program_id(0) == 0)
    def _():
        acc_ref[...] = jnp.zeros_like(acc_ref)
        sum_ref[...] = jnp.zeros_like(sum_ref)

    dq = jnp.concatenate([ref[0] for ref in dq_refs], 0)
    acc_ref[...] += dot(nt_ref[0], dq)
    gp = dot_nt(gpq_ref[0], w_ref[...]) * (1.0 / SEG)
    sum_ref[0:1] += col_sum(gp * ns_ref[0])
    sum_ref[1:2] += col_sum(gp) * SEG
    sum_ref[2:3] += col_sum(dq.astype(f32))


def shared_frames(main, from_left, from_right):
    t = main.shape[0]
    first = (main[:HR].astype(f32) + from_left.astype(f32)).astype(bf16)
    last = (main[t - 32 :].astype(f32) + from_right.astype(f32)).astype(bf16)
    return jnp.concatenate([first, main[HR : t - 32], last], 0)


def key_weights_kernel(
    nt_ref,
    dk_ref,
    dv_ref,
    fr_ref,
    fl_ref,
    gain_ref,
    bias_ref,
    sum_ref,
    pooled_ref,
    gpq_ref,
    memory_ref,
    dm_ref,
    summary_ref,
    gm_ref,
    vec_ref,
    upb_ref,
    w_hbm,
    accq_hbm,
    outg_hbm,
    bit_ref,
    keep_ref,
    send_ref,
    acc_s,
    cs_s,
    grads_s,
    norm_s,
    w_ref,
    accq_ref,
    outg_ref,
    sems,
):
    row = pl.program_id(0)
    late = ((w_hbm, w_ref), (accq_hbm, accq_ref), (outg_hbm, outg_ref))
    loads = [pltpu.make_async_copy(src, dst, sems.at[i]) for i, (src, dst) in enumerate(late)]

    @pl.when(row == 0)
    def _():
        for load in loads:
            load.start()
        acc_s[...] = jnp.zeros_like(acc_s)
        cs_s[...] = jnp.zeros_like(cs_s)

    for ref, cols in ((dk_ref, slice(0, D)), (dv_ref, slice(D, 2 * D))):
        d = shared_frames(ref[0], fl_ref[0, :, cols], fr_ref[0, :, cols])
        acc_s[:, cols] += dot(nt_ref[0], d)
        cs_s[:, cols] += col_sum(d.astype(f32))

    @pl.when(row == pl.num_programs(0) - 1)
    def _():
        for load in loads:
            load.wait()
        sums = sum_ref[...]
        norm = jnp.concatenate([gain_ref[0:1], bias_ref[0:1], jnp.zeros((126, D), f32)], 0).T
        norm_s[0] = jnp.broadcast_to(norm[:, 0:1], (D, 128))
        norm_s[1] = jnp.broadcast_to(norm[:, 1:2], (D, 128))
        norm_s[2:] = jnp.zeros((2, D, 128), f32)
        for part, (acc_ref, cs, left, right) in enumerate(
            (
                (accq_ref, sums[2:3], pooled_ref[...], gpq_ref[...]),
                (acc_s.at[:, :D], cs_s[:, :D], memory_ref[...], dm_ref[:, :D]),
                (acc_s.at[:, D:], cs_s[:, D:], memory_ref[...], dm_ref[:, D:]),
            )
        ):
            cols = slice(part * D, (part + 1) * D)
            grads_s[...] = dot_tn(left, right)
            for block in row_blocks(D, 128):
                for c0 in range(0, D, 128):
                    lanes = slice(c0, c0 + 128)
                    acc = acc_ref[block, lanes]
                    w = w_ref[block, part * D + c0 : part * D + c0 + 128].astype(f32)
                    grads_s[block, lanes] += acc * norm_s[0, block] + norm_s[1, block] * cs[:, lanes]
                    norm_s[2, block] += w * acc
                    norm_s[3, block] += w * cs[:, lanes]
            split_halves(bit_ref, keep_ref, send_ref, cols, grads_s)
        grads_s[...] = outg_ref[...] + dot_tn(summary_ref[...], gm_ref[...])
        split_halves(bit_ref, keep_ref, send_ref, slice(3 * D, 4 * D), grads_s)
        v = vec_ref[...]
        vectors = [sums[0:1], sums[1:2], v[0:1], v[1:2]]
        vectors += [sums[2:3] + col_sum(gpq_ref[...].astype(f32)), cs_s[:, D:] + col_sum(dm_ref[:, D:].astype(f32))]
        vectors += [v[2:3] + col_sum(gm_ref[...].astype(f32)), v[3:4]]
        hidden = [upb_ref[:, i * D : (i + 1) * D] for i in range(upb_ref.shape[1] // D)]
        packed = vectors + hidden + [jnp.zeros((128 - len(vectors) - len(hidden), D), f32)]
        columns = jnp.concatenate(packed, 0).T
        lane = lax.broadcasted_iota(jnp.int32, columns.shape, 1)
        gain_col = jnp.sum(norm_s[2], axis=-1, keepdims=True)
        bias_col = jnp.sum(norm_s[3], axis=-1, keepdims=True)
        columns += jnp.where(lane == 0, gain_col, jnp.where(lane == 1, bias_col, 0.0))
        grads_s[:, :128] = columns
        split_halves(bit_ref, keep_ref, send_ref, slice(4 * D, 4 * D + 128), grads_s.at[:, :128])


def own_frames_kernel(count, x_ref, *refs):
    dq_refs = refs[:count]
    dk_ref, dv_ref, fr_ref, fl_ref, gpq_ref, gmix_ref, gain_ref, w_ref, fg_ref, gy_s = refs[count:]
    t = x_ref.shape[1]
    gp = (dot_nt(gpq_ref[0], w_ref[:, :D]) * (1.0 / SEG))[: t // SEG]
    spread = jnp.broadcast_to(gp[:, None, :], (t // SEG, SEG, D)).reshape(t, D)
    dq = jnp.concatenate([ref[0] for ref in dq_refs], 0)
    dk = shared_frames(dk_ref[0], fl_ref[0, :, :D], fr_ref[0, :, :D])
    dv = shared_frames(dv_ref[0], fl_ref[0, :, D:], fr_ref[0, :, D:])
    gy_s[...] = (
        dot_nt(dq, w_ref[:, :D]) + dot_nt(dk, w_ref[:, D : 2 * D]) + dot_nt(dv, w_ref[:, 2 * D :]) + spread
    )
    for rows in row_blocks(t, 32):
        n, r = normalize(x_ref[0, rows].astype(f32))
        fg_ref[0, rows] = (gmix_ref[0, rows].astype(f32) + norm_back(gy_s[rows], n, r, gain_ref[0:1])).astype(bf16)


def halves(bit_ref, mine_ref, other_ref, cols):
    first = jnp.where(bit_ref[0] == 0, mine_ref[:, cols], other_ref[:, cols])
    second = jnp.where(bit_ref[0] == 0, other_ref[:, cols], mine_ref[:, cols])
    return jnp.concatenate([first, second], 0).astype(f32)


def unpack_ff_kernel(bit_ref, mine_u, other_u, mine_d, other_d, up_ref, down_ref):
    up_ref[...] = halves(bit_ref, mine_u, other_u, slice(None))
    down_ref[...] = halves(bit_ref, mine_d, other_d, slice(None)).T


def unpack_own_kernel(side_ref, part_ref, qkv_ref, out_ref):
    step = pl.program_id(0)

    @pl.when(step < 3)
    def _():
        qkv_ref[...] = part_ref[...].astype(f32)

    @pl.when(step == 3)
    def _():
        out_ref[...] = part_ref[...].astype(f32)


def unpack_rest_kernel(
    side_ref,
    part_ref,
    mine_v,
    other_v,
    qkv_in,
    out_in,
    qkv_ref,
    out_ref,
    gain_ref,
    bias_ref,
    qvb_ref,
    outb_ref,
    upb_ref,
    downb_ref,
):
    unpack_own_kernel(side_ref, part_ref, qkv_ref, out_ref)

    @pl.when(pl.program_id(0) == 0)
    def _():
        second = side_ref[0] == 1
        first = jnp.where(second, mine_v[...], other_v[...])
        last = jnp.where(second, other_v[...], mine_v[...])
        v = jnp.concatenate([first, last], 0).astype(f32).T
        gain_ref[0:1], gain_ref[1:2] = v[0:1], v[2:3]
        bias_ref[0:1], bias_ref[1:2] = v[1:2], v[3:4]
        qvb_ref[...] = v[4:6]
        outb_ref[...] = v[6:7]
        downb_ref[...] = v[7:8]
        for i in range(upb_ref.shape[1] // D):
            upb_ref[:, i * D : (i + 1) * D] = v[8 + i : 9 + i]


def shifted(value, axis, steps):
    count = lax.axis_size(axis)
    first, last = max(0, -steps), min(count, count - steps)
    return lax.ppermute(value, axis, [(source, source + steps) for source in range(first, last)])


class Exchange:
    def __init__(self):
        self.count_dp, self.count_tm = lax.axis_size("dp"), lax.axis_size("tm")
        dp, tm = lax.axis_index("dp"), lax.axis_index("tm")
        dp_bits = [(1 << b, 0) for b in range(self.count_dp.bit_length() - 1)]
        tm_bits = [(0, 1 << b) for b in range(self.count_tm.bit_length() - 1)]
        self.steps = [([tm_bits[0]], [tm_bits[0]])]
        self.steps += [([a], [b]) for a, b in zip(dp_bits, reversed(dp_bits))]
        self.steps += [(tm_bits[i : i + 2],) * 2 for i in range(1, len(tm_bits), 2)]
        self.digits = []
        for step in self.steps:
            digit = [0, 0]
            for parity in range(2):
                for f_dp, f_tm in step[parity]:
                    one = ((dp & f_dp) + (tm & f_tm) != 0).astype(jnp.int32)
                    digit[parity] = digit[parity] * 2 + one
            self.digits.append(jnp.where((tm & 1) == 0, digit[0], digit[1]))

    def radix(self, index):
        return 1 << len(self.steps[index][0])

    def send(self, part, index, flip=1):
        pairs = []
        for d in range(self.count_dp):
            for t in range(self.count_tm):
                to_d, to_t = d, t
                bits = self.steps[index][t & 1]
                for i, (f_dp, f_tm) in enumerate(bits):
                    if flip >> (len(bits) - 1 - i) & 1:
                        to_d, to_t = to_d ^ f_dp, to_t ^ f_tm
                pairs.append((d * self.count_tm + t, to_d * self.count_tm + to_t))
        return lax.ppermute(part, ("dp", "tm"), pairs)

    def total(self, terms):
        return sum(term.astype(f32) for term in terms).astype(bf16)

    def part(self, terms, index, flip):
        rows = terms[0].shape[0] // self.radix(index)
        start = (self.digits[index] ^ flip) * rows
        return [lax.dynamic_slice_in_dim(term, start, rows) for term in terms]

    def scatter(self, terms, index, sends=None):
        if sends is None:
            sends = [self.total(self.part(terms, index, flip)) for flip in range(1, self.radix(index))]
            terms = self.part(terms, index, 0)
        return terms, [self.send(value, index, flip + 1) for flip, value in enumerate(sends)]

    def gather(self, value, index):
        return [self.send(value, index, flip) for flip in range(1, self.radix(index))]

    def join(self, value, others, index):
        pieces = [value] + others
        out = jnp.concatenate(pieces, 0)
        for digit in range(1, len(pieces)):
            order = [pieces[place ^ digit] for place in range(len(pieces))]
            out = jnp.where(self.digits[index] == digit, jnp.concatenate(order, 0), out)
        return out


class Running:
    def __init__(self, exchange, keep, send):
        self.exchange = exchange
        self.steps = len(exchange.steps)
        self.last = 2 * self.steps - 1
        self.phase = 0
        self.terms, self.arriving = exchange.scatter([keep], 0, [send])
        self.value = None

    def index(self):
        return min(self.phase, self.last - self.phase)

    def beside(self, result):
        self.arriving, _ = lax.optimization_barrier((self.arriving, result))

    def before(self, operand):
        self.arriving, operand = lax.optimization_barrier((self.arriving, operand))
        return operand

    def advance(self):
        if self.phase < self.steps:
            self.terms = self.terms + self.arriving
        else:
            self.value = self.exchange.join(self.value, self.arriving, self.index())
        self.phase += 1
        if self.phase < self.steps:
            self.terms, self.arriving = self.exchange.scatter(self.terms, self.phase)
        else:
            if self.phase == self.steps:
                self.value = self.exchange.total(self.terms)
            self.arriving = self.exchange.gather(self.value, self.index())

    def along(self, result, operand):
        if self.phase < self.last:
            self.beside(result)
            operand = self.before(operand)
            self.advance()
        return operand


def sds(shape, dtype):
    return jax.ShapeDtypeStruct(shape, dtype)


def local(
    frames,
    lengths,
    norm_gain,
    norm_bias,
    qkv_weight,
    qv_bias,
    out_weight,
    out_bias,
    up_weight,
    up_bias,
    down_weight,
    down_bias,
    cotangent,
):
    micro, utts, t, _ = frames.shape
    rows = micro * utts
    segments = t // SEG
    sp = -(-segments // 16) * 16
    groups = t // GQ
    ext = HL + t + HR
    own_keys = ext - OWN0
    ff = up_weight.shape[1]
    tokens = rows * t
    total = t * lax.axis_size("tm")
    x = frames.reshape(rows, t, D)
    c = cotangent.reshape(rows, t, D)
    ob = out_bias.reshape(1, D)
    ub = up_bias.reshape(1, ff)
    db = down_bias.reshape(1, D)
    exchange = Exchange()
    steps = len(exchange.steps)
    bit = exchange.digits[0].reshape(1)

    pool = np.zeros((sp, t), np.float32)
    for s in range(segments):
        pool[s, s * SEG : (s + 1) * SEG] = 1
    poolh = np.zeros((16, HL), np.float32)
    for s in range(HL // SEG):
        poolh[16 - HL // SEG + s, s * SEG : (s + 1) * SEG] = 1
    expand = np.zeros((groups * MEMK, 16 + sp), np.float32)
    fold = np.zeros((sp, groups * MEMK), np.float32)
    for g in range(groups):
        for j in range(2 * MEMS - 1):
            seg = GROUP * g - MEMS + j
            expand[g * MEMK + j, 16 + seg] = 1
            if seg >= 0:
                fold[seg, g * MEMK + j] = 1
    place = np.zeros((sp, 16), np.float32)
    for j in range(MEMS):
        place[segments - MEMS + j, j] = 1
    hm8 = (np.arange(D)[None, :] // HD == np.arange(HEADS)[:, None]).astype(np.float32)
    hm4 = np.zeros((8, 256), np.float32)
    hm4[:4] = hm8[:4, :256]
    inside = np.zeros((KEYS, 128), np.float32)
    for lane in range(128):
        s = lane % GQ // SEG
        inside[s : s + MEMS, lane] = 1
        first = MEMK + 32 + s * SEG - LEFT
        inside[first : first + LEFT + SEG + RC, lane] = 1
    pool, poolh, expand, fold, place, hm8, hm4 = (
        jnp.asarray(v, bf16) for v in (pool, poolh, expand, fold, place, hm8, hm4)
    )
    inside = jnp.asarray(inside)

    pieces = []
    hop, need = 1, HL
    while need > 0:
        take = min(t, need)
        pieces.insert(0, shifted(x[:, t - take :], "tm", hop))
        need -= take
        hop += 1
    xl = jnp.concatenate(pieces, 1)
    xr = shifted(x[:, :HR], "tm", -1)

    q, k, v, nt, ns, pooled, pq = pl.pallas_call(
        own_kernel,
        grid=(rows,),
        in_specs=[
            row_spec((t, D)),
            const_spec((2, D)),
            const_spec((2, D)),
            const_spec((D, 3 * D)),
            const_spec((2, D)),
            const_spec((sp, t)),
        ],
        out_specs=[
            row_spec((t, D)),
            row_spec((ext, D)),
            row_spec((ext, D)),
            row_spec((D, t)),
            row_spec((sp, D)),
            row_spec((sp, D)),
            row_spec((sp, D)),
        ],
        out_shape=[
            sds((rows, t, D), bf16),
            sds((rows, ext, D), bf16),
            sds((rows, ext, D), bf16),
            sds((rows, D, t), bf16),
            sds((rows, sp, D), f32),
            sds((rows, sp, D), bf16),
            sds((rows, sp, D), bf16),
        ],
        scratch_shapes=[pltpu.VMEM((t, D), bf16), pltpu.VMEM((t, D), bf16)],
        compiler_params=params(),
        cost_estimate=cost(),
        name="own",
    )(x, norm_gain, norm_bias, qkv_weight, qv_bias, pool)

    any_spec = pl.BlockSpec(memory_space=pl.ANY)
    after_first = lambda r: (jnp.maximum(r - 1, 0), 0, 0)
    kext, vext, mkg, mvg, summary, memory, ps, p, attended = pl.pallas_call(
        functools.partial(memory_kernel, groups, total, utts),
        grid=(1 + rows,),
        in_specs=[
            smem_spec(),
            const_spec((rows, HL, D)),
            const_spec((rows, HR, D)),
            const_spec((rows, sp, D)),
            const_spec((2, D)),
            const_spec((2, D)),
            const_spec((D, 3 * D)),
            const_spec((2, D)),
            const_spec((D, D)),
            const_spec((1, D)),
            const_spec((16, HL)),
            const_spec((groups * MEMK, 16 + sp)),
            const_spec((HEADS, D)),
            any_spec,
            any_spec,
            pl.BlockSpec((1, t, D), after_first),
            const_spec((8, 256)),
            const_spec((KEYS, 128)),
        ],
        out_specs=[any_spec] * 7
        + [
            pl.BlockSpec((1, groups, KEYS, HEADS * GQ), lambda r: (jnp.maximum(r - 1, 0), 0, 0, 0)),
            pl.BlockSpec((1, t, D), after_first),
        ],
        out_shape=[
            sds((rows, ext, D), bf16),
            sds((rows, ext, D), bf16),
            sds((rows, groups * MEMK, D), bf16),
            sds((rows, groups * MEMK, D), bf16),
            sds((rows, sp, D), bf16),
            sds((rows, sp, D), bf16),
            sds((rows, own_keys, HEADS * sp), bf16),
            sds((rows, groups, KEYS, HEADS * GQ), bf16),
            sds((rows, t, D), bf16),
        ],
        scratch_shapes=[
            pltpu.VMEM((rows, ext, D), bf16),
            pltpu.VMEM((rows, ext, D), bf16),
            pltpu.VMEM((4, max(own_keys, HALO), HEADS * sp), f32),
            pltpu.VMEM((4, max(own_keys, HALO), HEADS * sp), bf16),
            pltpu.VMEM((rows, groups * MEMK, D), bf16),
            pltpu.VMEM((rows, groups * MEMK, D), bf16),
            pltpu.VMEM((rows, sp, D), bf16),
            pltpu.VMEM((rows, sp, D), bf16),
            pltpu.VMEM((rows, own_keys, HEADS * sp), bf16),
            pltpu.SemaphoreType.DMA((2,)),
            pltpu.SemaphoreType.DMA((4,)),
            pltpu.SemaphoreType.DMA((5,)),
        ],
        input_output_aliases={13: 0, 14: 1},
        compiler_params=params(),
        cost_estimate=cost(),
        name="attend",
    )(
        lengths,
        xl,
        xr,
        pq,
        norm_gain,
        norm_bias,
        qkv_weight,
        qv_bias,
        out_weight,
        ob,
        poolh,
        expand,
        hm8,
        k,
        v,
        q,
        hm4,
        inside,
    )

    tb = min(512, tokens)
    tiles = 8
    wide = ff // tiles
    token_spec = pl.BlockSpec((tb, D), lambda i: (i, 0))
    out, gmix, gatt, ff_keep, ff_send, outg, vec, upb = pl.pallas_call(
        functools.partial(ff_kernel, tiles),
        grid=(tokens // tb,),
        in_specs=[
            smem_spec(),
            token_spec,
            token_spec,
            token_spec,
            const_spec((2, D)),
            const_spec((2, D)),
            const_spec((D, D)),
            const_spec((1, D)),
            const_spec((D, ff)),
            const_spec((1, ff)),
            const_spec((ff, D)),
            const_spec((1, D)),
        ],
        out_specs=[
            token_spec,
            token_spec,
            token_spec,
            const_spec((D // 2, 2 * ff)),
            const_spec((D // 2, 2 * ff)),
            const_spec((D, D)),
            const_spec((8, D)),
            const_spec((1, ff)),
        ],
        out_shape=[
            sds((tokens, D), bf16),
            sds((tokens, D), bf16),
            sds((tokens, D), bf16),
            sds((D // 2, 2 * ff), bf16),
            sds((D // 2, 2 * ff), bf16),
            sds((D, D), f32),
            sds((8, D), f32),
            sds((1, ff), f32),
        ],
        scratch_shapes=[
            pltpu.VMEM((tb, D), f32),
            pltpu.VMEM((tb, 128), f32),
            pltpu.VMEM((tb, D), bf16),
            pltpu.VMEM((D + 16, tb), bf16),
            pltpu.VMEM((D, tb), bf16),
            pltpu.VMEM((tb, wide), f32),
            pltpu.VMEM((tb, wide), f32),
            pltpu.VMEM((tb, wide), bf16),
            pltpu.VMEM((tb, wide), bf16),
            pltpu.VMEM((tb, 2 * wide), bf16),
            pltpu.VMEM((tb, 2 * wide), bf16),
            pltpu.VMEM((tb, 2 * wide), bf16),
            pltpu.VMEM((tb, 2 * wide), bf16),
            pltpu.VMEM((tb, D), f32),
            pltpu.VMEM((tb, D), f32),
            pltpu.VMEM((D, ff), f32),
            pltpu.VMEM((D, ff), f32),
        ],
        compiler_params=params(),
        cost_estimate=cost(),
        name="feed_forward",
    )(
        bit,
        x.reshape(tokens, D),
        c.reshape(tokens, D),
        attended.reshape(tokens, D),
        norm_gain,
        norm_bias,
        out_weight,
        ob,
        up_weight,
        ub,
        down_weight,
        db,
    )
    gatt = gatt.reshape(rows, t, D)

    ff_sum = Running(exchange, ff_keep, ff_send)

    cut = groups * 2 // 8
    parts = [(0, cut), (cut, groups)] if cut else [(0, groups)]
    dqs, dks, dvs, dms = [], [], [], []
    for g0, g1 in parts:
        near = (g1 - g0) * GQ + NEAR - GQ
        if g0:
            gatt = ff_sum.along(dq, gatt)
        held = groups // 2 if g1 <= groups // 2 else groups
        dq, dk, dv, dm, first = pl.pallas_call(
            functools.partial(attend_back_kernel, g0, g1),
            grid=(rows,),
            in_specs=[
                row_spec((held * GQ, D)),
                row_spec((ext, D)),
                row_spec((ext, D)),
                row_spec((groups * MEMK, D)),
                row_spec((groups * MEMK, D)),
                row_spec((held, KEYS, HEADS * GQ)),
                row_spec((held * GQ, D)),
                const_spec((8, 256)),
            ],
            out_specs=[
                row_spec(((g1 - g0) * GQ, D)),
                row_spec((near, D)),
                row_spec((near, D)),
                row_spec(((g1 - g0) * MEMK, 2 * D)),
                row_spec((MEMK, 2 * D)),
            ],
            out_shape=[
                sds((rows, (g1 - g0) * GQ, D), bf16),
                sds((rows, near, D), bf16),
                sds((rows, near, D), bf16),
                sds((rows, (g1 - g0) * MEMK, 2 * D), bf16),
                sds((rows, MEMK, 2 * D), bf16),
            ],
            scratch_shapes=[pltpu.VMEM((near, D), f32), pltpu.VMEM((near, D), f32)],
            compiler_params=params(),
            cost_estimate=cost(),
            name="attend_back",
        )(q, kext, vext, mkg, mvg, p, gatt, hm4)
        for group, value in zip((dqs, dks, dvs, dms), (dq, dk, dv, dm)):
            group.append(value)
        if g0 == 0:
            recv = shifted(first, "tm", -1)

    recv = ff_sum.along(dq, recv)
    dko, dvo, left, right, gpq, dm, gm = pl.pallas_call(
        functools.partial(memory_back_kernel, parts),
        grid=(1,),
        in_specs=[const_spec(v.shape) for v in dms]
        + [any_spec] * (2 * len(parts))
        + [
            const_spec((rows, MEMK, 2 * D)),
            const_spec((sp, groups * MEMK)),
            const_spec((sp, MEMK)),
            const_spec((D, 3 * D)),
            const_spec((D, D)),
            const_spec((HEADS, D)),
            const_spec((rows, sp, D)),
            any_spec,
            any_spec,
            any_spec,
        ],
        out_specs=[
            any_spec,
            any_spec,
            const_spec((rows, 32, 2 * D)),
            const_spec((rows, HR, 2 * D)),
            const_spec((rows, sp, D)),
            const_spec((rows, sp, 2 * D)),
            const_spec((rows, sp, D)),
        ],
        out_shape=[
            sds((rows, t, D), bf16),
            sds((rows, t, D), bf16),
            sds((rows, 32, 2 * D), bf16),
            sds((rows, HR, 2 * D), bf16),
            sds((rows, sp, D), bf16),
            sds((rows, sp, 2 * D), bf16),
            sds((rows, sp, D), bf16),
        ],
        scratch_shapes=[
            pltpu.VMEM((rows, own_keys, D), bf16),
            pltpu.VMEM((rows, own_keys, D), bf16),
            pltpu.VMEM((rows, own_keys, HEADS * sp), bf16),
            pltpu.VMEM((rows, own_keys, HEADS * sp), f32),
            pltpu.VMEM((rows, own_keys, HEADS * sp), bf16),
            pltpu.VMEM((rows, own_keys, D), f32),
            pltpu.VMEM((rows, own_keys, D), f32),
            pltpu.VMEM((rows, t, D), bf16),
            pltpu.VMEM((rows, t, D), bf16),
        ]
        + [pltpu.VMEM(v.shape, bf16) for v in dks + dvs]
        + [pltpu.SemaphoreType.DMA((rows, 3 + 2 * len(parts))), pltpu.SemaphoreType.DMA((rows, 2))],
        compiler_params=params(),
        cost_estimate=cost(),
        name="memory_back",
    )(*dms, *dks, *dvs, recv, fold, place, qkv_weight, out_weight, hm8, pq, kext, vext, ps)

    from_right = shifted(left, "tm", -1)
    from_left = shifted(right, "tm", 1)
    gpq = ff_sum.along(gpq, gpq)
    dq_specs = [row_spec(v.shape[1:]) for v in dqs]
    accq, sums = pl.pallas_call(
        functools.partial(query_weights_kernel, len(dqs)),
        grid=(rows,),
        in_specs=[row_spec((D, t)), row_spec((sp, D))] + dq_specs + [row_spec((sp, D)), const_spec((D, D))],
        out_specs=[const_spec((D, D)), const_spec((8, D))],
        out_shape=[sds((D, D), f32), sds((8, D), f32)],
        compiler_params=params(),
        cost_estimate=cost(),
        name="query_weights",
    )(nt, ns, *dqs, gpq, qkv_weight)

    sums = ff_sum.along(sums, sums)
    keep, send = pl.pallas_call(
        key_weights_kernel,
        grid=(rows,),
        in_specs=[
            row_spec((D, t)),
            row_spec((t, D)),
            row_spec((t, D)),
            row_spec((32, 2 * D)),
            row_spec((HR, 2 * D)),
            const_spec((2, D)),
            const_spec((2, D)),
            const_spec((8, D)),
            const_spec((rows * sp, D)),
            const_spec((rows * sp, D)),
            const_spec((rows * sp, D)),
            const_spec((rows * sp, 2 * D)),
            const_spec((rows * sp, D)),
            const_spec((rows * sp, D)),
            const_spec((8, D)),
            const_spec((1, ff)),
            any_spec,
            any_spec,
            any_spec,
            smem_spec(),
        ],
        out_specs=[pl.BlockSpec(memory_space=pltpu.VMEM)] * 2,
        out_shape=[in_vmem((D // 2, 4 * D + 128), bf16)] * 2,
        scratch_shapes=[
            pltpu.VMEM((D, 2 * D), f32),
            pltpu.VMEM((1, 2 * D), f32),
            pltpu.VMEM((D, D), f32),
            pltpu.VMEM((4, D, 128), f32),
            pltpu.VMEM((D, 3 * D), bf16),
            pltpu.VMEM((D, D), f32),
            pltpu.VMEM((D, D), f32),
            pltpu.SemaphoreType.DMA((3,)),
        ],
        compiler_params=params(56),
        cost_estimate=cost(),
        name="key_weights",
    )(
        nt,
        dko,
        dvo,
        from_right,
        from_left,
        norm_gain,
        norm_bias,
        sums,
        pooled.reshape(rows * sp, D),
        gpq.reshape(rows * sp, D),
        memory.reshape(rows * sp, D),
        dm.reshape(rows * sp, 2 * D),
        summary.reshape(rows * sp, D),
        gm.reshape(rows * sp, D),
        vec,
        upb,
        qkv_weight,
        accq,
        outg,
        bit,
    )
    ff_sum.beside(send)
    send = ff_sum.before(send)
    rest = Running(exchange, keep, send)
    gpq = rest.before(gpq)
    fg = pl.pallas_call(
        functools.partial(own_frames_kernel, len(dqs)),
        grid=(rows,),
        in_specs=[row_spec((t, D))]
        + dq_specs
        + [
            row_spec((t, D)),
            row_spec((t, D)),
            row_spec((32, 2 * D)),
            row_spec((HR, 2 * D)),
            row_spec((sp, D)),
            row_spec((t, D)),
            const_spec((2, D)),
            const_spec((D, 3 * D)),
        ],
        out_specs=row_spec((t, D)),
        out_shape=sds((rows, t, D), bf16),
        scratch_shapes=[pltpu.VMEM((t, D), f32)],
        compiler_params=params(56),
        cost_estimate=cost(),
        name="own_frames",
    )(x, *dqs, dko, dvo, from_right, from_left, gpq, gmix.reshape(rows, t, D), norm_gain, qkv_weight)
    turns = [steps - 2, steps - 1, steps + 1] if ff_sum.last - ff_sum.phase <= 3 else list(range(1, 2 * steps - 1))
    while rest.phase < rest.last:
        if rest.phase == 1:
            rest.beside(fg)
        if rest.phase in turns and ff_sum.phase < ff_sum.last:
            ff_sum.arriving, rest.arriving = lax.optimization_barrier((ff_sum.arriving, rest.arriving))
            ff_sum.advance()
        if rest.phase == rest.last - 1:
            blocks = ff // D
            half = D // 2
            up_sum, down_sum = pl.pallas_call(
                unpack_ff_kernel,
                grid=(blocks,),
                in_specs=[smem_spec()]
                + [pl.BlockSpec((half, D), lambda i: (0, i))] * 2
                + [pl.BlockSpec((half, D), lambda i: (0, i + blocks))] * 2,
                out_specs=[pl.BlockSpec((D, D), lambda i: (0, i)), pl.BlockSpec((D, D), lambda i: (i, 0))],
                out_shape=[sds((D, ff), f32), sds((ff, D), f32)],
                compiler_params=params(28),
                cost_estimate=cost(),
                name="unpack_feed_forward",
            )(bit, ff_sum.value, ff_sum.arriving[0], ff_sum.value, ff_sum.arriving[0])
            rest.beside(up_sum)
        rest.advance()
    grads, other = rest.value, rest.arriving[0]
    half = D // 2
    part_spec = pl.BlockSpec((half, D), lambda i, side: (0, i))
    vector_spec = pl.BlockSpec((half, 128), lambda i, side: (0, 4 * D // 128), pipeline_mode=pl.Buffered(1))
    big_specs = [
        pl.BlockSpec((half, D), lambda i, side: (side[0], jnp.minimum(i, 2))),
        pl.BlockSpec((half, D), lambda i, side: (side[0], 0)),
    ]
    big_shapes = [sds((D, 3 * D), f32), sds((D, D), f32)]
    qkv_sum, out_sum = pl.pallas_call(
        unpack_own_kernel,
        grid_spec=pltpu.PrefetchScalarGridSpec(
            num_scalar_prefetch=1, grid=(4,), in_specs=[part_spec], out_specs=big_specs
        ),
        out_shape=big_shapes,
        compiler_params=params(28),
        cost_estimate=cost(),
        name="unpack_own",
    )(bit, grads)
    small_shapes = [(2, D), (2, D), (2, D), (1, D), (1, ff), (1, D)]
    other, qkv_sum = lax.optimization_barrier((other, qkv_sum))
    qkv_sum, out_sum, gain_sum, bias_sum, qvb_sum, outb_sum, upb_sum, downb_sum = pl.pallas_call(
        unpack_rest_kernel,
        grid_spec=pltpu.PrefetchScalarGridSpec(
            num_scalar_prefetch=1,
            grid=(4,),
            in_specs=[part_spec, vector_spec, vector_spec, any_spec, any_spec],
            out_specs=big_specs
            + [pl.BlockSpec(v, lambda i, side: (0, 0), pipeline_mode=pl.Buffered(1)) for v in small_shapes],
        ),
        out_shape=big_shapes + [sds(v, f32) for v in small_shapes],
        input_output_aliases={4: 0, 5: 1},
        compiler_params=params(28),
        cost_estimate=cost(),
        name="unpack_rest",
    )(1 - bit, other, grads, other, qkv_sum, out_sum)
    return (
        out.reshape(micro, utts, t, D),
        fg.reshape(micro, utts, t, D),
        gain_sum,
        bias_sum,
        qkv_sum,
        qvb_sum,
        out_sum,
        outb_sum.reshape(D),
        up_sum,
        upb_sum.reshape(ff),
        down_sum,
        downb_sum.reshape(D),
    )


def solution(mesh):
    spread = P(None, "dp", "tm", None)
    in_specs = (spread, P("dp")) + (P(),) * 10 + (spread,)
    out_specs = (spread, spread) + (P(),) * 10
    return jax.shard_map(local, mesh=mesh, in_specs=in_specs, out_specs=out_specs, check_vma=False)
```
